256 devices in a mesh: dp: 16 (over x, y), expert: 16 (over z, core).
Axes of the slice: x: 4, y: 4, z: 8, core: 2. Of those that a mesh axis runs over, the one named last changes fastest.
Arguments:
- out_grad: bfloat16 [32768, 2048], P(('dp', 'expert')), may hold values from -5 to 5
- saved_hidden: bfloat16 [32768, 8, 384], P(('dp', 'expert')), may hold values from -6 to 6
- gate_weight: bfloat16 [32768, 8], P(('dp', 'expert')), may hold values from 0.19921875 to 1
- expert_ids: int32 [32768, 8], P(('dp', 'expert')), may hold values from 0 to 63, all different within a row; in each aligned block of 128 rows (0 to 127, 128 to 255, ...) at most 24 rows name the same one
- down_weight: bfloat16 [2048, 64, 384], P('dp', 'expert'), may hold values from -0.3125 to 0.3125
Outputs:
- grad_hidden: bfloat16 [32768, 8, 384], P(('dp', 'expert'))
- grad_gate: bfloat16 [32768, 8], P(('dp', 'expert'))
- grad_down: float32 [2048, 64, 384], P('dp', 'expert')
The draws below stay inside these ranges and needn't reach their ends.
Inputs may be any that keep to these rules, and one draw needn't show every extreme that they name: `expert_ids`: each token names 8 different experts. Among the tokens of one device no expert is named by more than 24 tokens, and in every draw some expert is named by exactly 24 tokens of some device.
All inputs are finite; a program needn't handle non-finite values.
Results may differ from the reference program's by a relative error of at most 0.014.
Values may be sent and summed in bfloat16 or wider, within the bound.
No kernel may reach another device: no remote copies, remote signals or barrier semaphores. Data moves between devices by JAX's collectives and lax.ppermute only.
A program may use at most 128 MiB of HBM per device.

```python
import math
import jax
import jax.numpy as jnp
import numpy as np
from jax import lax

D = 2048
FF = 384
TOPK = 8
TOK_DEV = 128
EXPERTS = 64
TOKENS = 32768
CAP = 24
N_DP = 16
N_EXPERT = 16


def with_spikes(values, rng, source, target, parts, factor):
    owner, partner = [(jnp.arange(values.shape[dim]) // (values.shape[dim] // parts)).reshape([-1 if axis == dim else 1 for axis in range(values.ndim)]) for dim in (source, target)]
    chosen = jax.random.permutation(rng, parts)[partner]
    strong = (owner == chosen) | (owner == (partner + parts // 2) % parts)
    return jnp.where(strong, factor * values, values)


def shard_levels(stream_key, extent, split, least, top_value):
    loudness = 1.0
    for position, blocks in split:
        steps = jax.random.uniform(jax.random.fold_in(jax.random.fold_in(stream_key, 6), position), (blocks,), jnp.float32, least / len(split), top_value / len(split))
        loudness = loudness * jnp.repeat(jnp.exp(steps), extent[position] // blocks).reshape((-1,) + (1,) * (len(extent) - 1 - position))
    return loudness


def deal_out(own_key, own, number, rows, number_of, top, bound, slope):
    order = jax.random.permutation(own_key, number_of)
    heavy_load, usual = shares(number_of, rows * top, bound, slope, True), shares(number_of, rows * top, bound, slope, False)
    places = jnp.arange(number_of)

    def named(lengths, rotation):
        used = int((lengths > 0).sum())
        fixed = max(1, used // 4)
        passed = fixed + (places - fixed + rotation * (used - fixed)) % max(1, number_of - fixed)
        return jnp.zeros((number_of,), jnp.int32).at[order[jnp.where(places < fixed, places, passed)]].set(jnp.asarray(lengths, jnp.int32))

    lengths = jnp.where(number % 4 == 0, named(heavy_load, number // 4), named(usual, number - number // 4 - 1))
    mixed = jax.random.permutation(jax.random.fold_in(own, 3), number_of)
    donor, sink = mixed[0:number_of // 2 * 2:2], mixed[1:number_of // 2 * 2:2]
    room = jnp.minimum(lengths[donor] - 1, bound - lengths[sink]) // 2
    room = jnp.where((donor == order[0]) | (sink == order[0]) | (lengths[sink] == 0), 0, jnp.maximum(room, 0))
    passed = jax.random.randint(jax.random.fold_in(own, 4), (number_of // 2,), 0, 1 << 20) % (room + 1)
    lengths = lengths.at[donor].add(-passed).at[sink].add(passed)
    members = jnp.searchsorted(jnp.cumsum(lengths), jnp.arange(rows * top), side="right").astype(jnp.int32)
    table = members.reshape(top, rows).T
    table = table[jax.random.permutation(jax.random.fold_in(own, 1), rows)]
    rotation = jax.random.randint(jax.random.fold_in(own, 2), (rows, 1), 0, top)
    return jnp.take_along_axis(table, (jnp.arange(top)[None, :] + rotation) % top, axis=1)


def shares(amount, total, most, slope, full):
    weights = [(1 << 20) // math.isqrt(standing ** slope) + 1 for standing in range(1, amount + 1)]
    largest = most if full else min(most, max(-(-total // amount), total * weights[0] // sum(weights)))
    least = 1 if total - largest >= amount - 1 else 0
    counts, rest = [largest] + [least] * (amount - 1), total - largest - least * (amount - 1)
    while rest > 0:
        movable = [i for i in range(1, amount) if counts[i] < largest] or [i for i in range(1, amount) if counts[i] < most]
        pool, budget = sum([weights[i] for i in movable]), rest
        for i in movable:
            more = min(most - counts[i], max(1, budget * weights[i] // pool), rest)
            counts[i] = counts[i] + more
            rest = rest - more
    return np.array(counts)


def scatter_about(own_key, shape, width, reach, pieces=(), kind=jnp.bfloat16):
    factor_of = shard_levels(own_key, shape, pieces, -0.22, 0.18) if pieces else 1.0
    entries = jax.random.normal(own_key, shape, jnp.float32) * width * factor_of
    return jnp.minimum(jnp.maximum(entries, -reach), reach).astype(kind)


def heavy_noise(stream_key, shape, width, most, shards, heavy, held_as=jnp.bfloat16):
    array = width * jax.random.normal(stream_key, shape, jnp.float32)
    if shards:
        array = array * shard_levels(stream_key, shape, shards, -0.22, 0.18)
    return jnp.clip(with_spikes(array, jax.random.fold_in(stream_key, 3), *heavy), -most, most).astype(held_as)


def setup_inputs(seed: int = 0) -> dict:
    arg_keys = jax.random.split(jax.random.key(seed), 6)
    out_grad = heavy_noise(arg_keys[0], (TOKENS, D), 0.2, 5.0, ((0, 256),), (0, 1, 256, 6.0))
    saved_hidden = scatter_about(arg_keys[1], (TOKENS, TOPK, FF), 1.0, 6.0, ((0, 256),))
    gate_weight = jnp.clip(jnp.exp(math.log(1.0) - 1.6133518 * jax.random.uniform(arg_keys[2], (TOKENS, TOPK), jnp.float32) ** shard_levels(arg_keys[2], (TOKENS, TOPK), ((0, 256),), -0.2, 0.2)), 0.19921875, 1.0).astype(jnp.bfloat16)
    expert_ids_keys = jax.random.split(jax.random.fold_in(arg_keys[3], 1), TOKENS // TOK_DEV)
    expert_ids_turns = jax.random.permutation(jax.random.fold_in(arg_keys[3], 3), TOKENS // TOK_DEV)
    expert_ids = jax.vmap(lambda own, number: deal_out(jax.random.fold_in(arg_keys[3], 2), own, number, TOK_DEV, EXPERTS, TOPK, CAP, 2))(expert_ids_keys, expert_ids_turns).reshape((TOKENS, TOPK))
    down_weight = scatter_about(arg_keys[4], (D, EXPERTS, FF), FF ** -0.5, 0.3125, ((0, 16), (1, 16)))
    return dict(out_grad=out_grad, saved_hidden=saved_hidden, gate_weight=gate_weight, expert_ids=expert_ids, down_weight=down_weight)


def reference(out_grad, saved_hidden, gate_weight, expert_ids, down_weight):
    route_count = TOKENS * TOPK
    limit = CAP * N_DP * N_EXPERT
    flat_ids = expert_ids.reshape(route_count).astype(jnp.int32)
    grad_pad = jnp.concatenate([out_grad, jnp.zeros((1, D), out_grad.dtype)], axis=0)
    hidden_pad = jnp.concatenate([saved_hidden.reshape(route_count, FF), jnp.zeros((1, FF), saved_hidden.dtype)], axis=0)
    gate_pad = jnp.concatenate([gate_weight.reshape(route_count), jnp.zeros((1,), gate_weight.dtype)], axis=0)

    def one_expert(expert):
        routes = jnp.nonzero(flat_ids == expert, size=limit, fill_value=route_count)[0].astype(jnp.int32)
        token_rows = jnp.where(routes < route_count, routes // TOPK, TOKENS).astype(jnp.int32)
        grad_rows = grad_pad[token_rows]
        hidden_rows = hidden_pad[routes]
        gate_rows = gate_pad[routes]
        scaled = (grad_rows.astype(jnp.float32) * gate_rows.astype(jnp.float32)[:, None]).astype(jnp.bfloat16)
        weight = lax.dynamic_index_in_dim(down_weight, expert, 1, keepdims=False)
        weight_grad = jnp.dot(scaled.T, hidden_rows, preferred_element_type=jnp.float32)
        hidden_grad = jnp.dot(scaled, weight, preferred_element_type=jnp.float32).astype(jnp.bfloat16)
        recomputed = jnp.dot(hidden_rows, weight.T, preferred_element_type=jnp.float32)
        gate_grad = jnp.sum(grad_rows.astype(jnp.float32) * recomputed, axis=1).astype(jnp.bfloat16)
        return routes, hidden_grad, gate_grad, weight_grad

    routes, hidden_grads, gate_grads, weight_grads = lax.map(one_expert, jnp.arange(EXPERTS, dtype=jnp.int32))
    flat_routes = routes.reshape(EXPERTS * limit)
    grad_hidden = jnp.zeros((route_count + 1, FF), jnp.bfloat16).at[flat_routes].set(hidden_grads.reshape(EXPERTS * limit, FF))
    grad_hidden = grad_hidden[:route_count].reshape(TOKENS, TOPK, FF)
    grad_gate = jnp.zeros((route_count + 1,), jnp.bfloat16).at[flat_routes].set(gate_grads.reshape(EXPERTS * limit))
    grad_gate = grad_gate[:route_count].reshape(TOKENS, TOPK)
    grad_down = jnp.transpose(weight_grads, (1, 0, 2))
    return grad_hidden, grad_gate, grad_down
```

```python
import functools

import jax
import jax.numpy as jnp
from jax import lax
from jax.experimental import pallas as pl
from jax.experimental.pallas import tpu as pltpu
from jax.sharding import PartitionSpec as P

CAP = 24
SIDE = 4
EXTRA = 8
BF16, F32, I32 = jnp.bfloat16, jnp.float32, jnp.int32


def iota(shape, dim):
    return lax.broadcasted_iota(I32, shape, dim)


def dot(a, b):
    return jnp.dot(a, b, preferred_element_type=F32)


def pack_kernel(owners, local, ids_ref, gate_ref, hidden_ref, wire_ref, pos_ref):
    top, tokens = ids_ref.shape
    routes, width = hidden_ref.shape
    experts = owners * local
    ids = ids_ref[...]
    expert_no = iota((experts, tokens), 0)
    named = [expert_no == ids[k : k + 1, :] for k in range(top)]
    member = sum(n.astype(F32) for n in named)
    earlier = (iota((tokens, tokens), 0) < iota((tokens, tokens), 1)).astype(F32).astype(BF16)
    before = dot(member.astype(BF16), earlier)
    pos = jnp.concatenate(
        [jnp.sum(jnp.where(n, before, 0.0), axis=0, keepdims=True) for n in named], axis=0
    )
    pos_ref[...] = pos
    spread = (iota((tokens, routes), 1) // top == iota((tokens, routes), 0)).astype(F32).astype(BF16)
    own = iota((top, routes), 1) % top == iota((top, routes), 0)

    def row(x):
        return jnp.sum(jnp.where(own, dot(x.astype(BF16), spread), 0.0), axis=0, keepdims=True)

    slot_row = row(ids.astype(F32)) * CAP + row(pos)
    gate_row = row(gate_ref[...].astype(F32))
    slots = jnp.where(member > 0.0, before, -1.0).astype(BF16)
    r, c = iota((owners * EXTRA, experts), 0), iota((owners * EXTRA, experts), 1)
    pick = ((r % EXTRA < local) & (c == r // EXTRA * local + r % EXTRA)).astype(F32).astype(BF16)
    slots = dot(pick, slots)
    slots = jnp.concatenate([slots, jnp.zeros((owners * EXTRA, width - tokens), F32)], axis=1)
    rows = local * CAP
    group = 4
    hidden = hidden_ref[...]
    for g in range(owners // group):
        row_no = (iota((group * rows, routes), 0) + g * group * rows).astype(F32)
        onehot = jnp.where(row_no == slot_row, gate_row, 0.0).astype(BF16)
        packed = dot(onehot, hidden)
        for i in range(group):
            o = g * group + i
            wire_ref[o] = jnp.concatenate(
                [packed[i * rows : (i + 1) * rows], slots[o * EXTRA : (o + 1) * EXTRA]], axis=0
            ).astype(BF16)


def place(first_is_x, a, b, xy_ref):
    dx, dy = (a, b) if first_is_x else (b, a)
    x, y = (xy_ref[0] + dx) % SIDE, (xy_ref[1] + dy) % SIDE
    return x * SIDE + y


def grad_down_kernel(local, xy_ref, wire_ref, grad_hbm, *refs):
    messages, x_hbm = refs[: local * SIDE], refs[local * SIDE]
    gbuf, xbuf, abuf, gsem, xsem, msem = refs[local * SIDE + 1 :]
    owners, tokens, model = grad_hbm.shape
    width = wire_ref.shape[2]
    pairs = owners // 2

    def load(p):
        return pltpu.make_async_copy(grad_hbm.at[pl.ds(2 * p, 2)], gbuf.at[pl.ds(2 * p, 2)], gsem.at[p])

    for p in range(pairs):
        load(p).start()
    wire = wire_ref[...].astype(F32)
    block = 2 * CAP
    for p in range(pairs):
        slot = [wire[2 * p + i, local * CAP : local * CAP + EXTRA, :tokens] for i in range(2)]
        slot[1] = jnp.where(slot[1] >= 0.0, slot[1] + CAP, -1.0)
        slot = jnp.concatenate(slot, axis=1)
        onehot = jnp.concatenate(
            [
                (slot[e : e + 1, :] == iota((block, 2 * tokens), 0).astype(F32)).astype(F32)
                for e in range(local)
            ],
            axis=0,
        ).astype(BF16)
        load(p).wait()
        rows = dot(onehot, gbuf[2 * p : 2 * p + 2].reshape(2 * tokens, model)).astype(BF16)
        for e in range(local):
            xbuf[e, p * block : (p + 1) * block, :] = rows[e * block : (e + 1) * block]
    copies = []
    for e in range(local):
        copies.append(pltpu.make_async_copy(xbuf.at[e], x_hbm.at[e], xsem.at[e]))
        copies[-1].start()
    for e in range(local):
        hidden = wire[:, e * CAP : (e + 1) * CAP, :].reshape(owners * CAP, width)
        hidden = hidden.T.astype(BF16)
        step = model // 4
        for n in range(4):
            abuf[e, :, n * step : (n + 1) * step] = dot(hidden, xbuf[e, :, n * step : (n + 1) * step]).astype(BF16)
        for a in range(SIDE):
            for b in range(SIDE):
                at = pl.multiple_of(place(e < local // 2, a, b, xy_ref) * 128, 128)
                copies.append(
                    pltpu.make_async_copy(
                        abuf.at[e, :, pl.ds(at, 128)], messages[e * SIDE + a].at[b], msem.at[e, a, b]
                    )
                )
                copies[-1].start()
    for c in copies:
        c.wait()


def hidden_kernel(local, xy_ref, x_hbm, *refs):
    pieces, out_ref = refs[: local * SIDE], refs[local * SIDE]
    xbuf, wbuf, ubuf, xsem, wsem = refs[local * SIDE + 1 :]
    owners, _, width = out_ref.shape
    depth = pieces[0].shape[1]
    copies = []
    for e in range(local):
        mine = [pltpu.make_async_copy(x_hbm.at[e], xbuf.at[e], xsem.at[e])]
        for a in range(SIDE):
            for b in range(SIDE):
                at = pl.multiple_of(place(e >= local // 2, a, b, xy_ref) * depth, depth)
                mine.append(
                    pltpu.make_async_copy(
                        pieces[e * SIDE + a].at[b], wbuf.at[e, pl.ds(at, depth), :], wsem.at[e, a, b]
                    )
                )
        for c in mine:
            c.start()
        copies.append(mine)
    for e in range(local):
        for c in copies[e]:
            c.wait()
        u = dot(xbuf[e], wbuf[e])
        ubuf[:, e * CAP : (e + 1) * CAP, :] = u.reshape(owners, CAP, width)
    out_ref[...] = ubuf[...].astype(BF16)


def unpack_kernel(ids_ref, pos_ref, gate_ref, hidden_ref, back_ref, out_ref, gate_out_ref):
    top, tokens = ids_ref.shape
    routes, width = hidden_ref.shape
    slots = back_ref.shape[0]
    spread = (iota((routes, tokens), 0) // top == iota((routes, tokens), 1)).astype(F32).astype(BF16)
    own = iota((routes, top), 0) % top == iota((routes, top), 1)

    def column(x):
        y = lax.dot_general(spread, x.astype(BF16), (((1,), (1,)), ((), ())), preferred_element_type=F32)
        return jnp.sum(jnp.where(own, y, 0.0), axis=1, keepdims=True)

    slot = column(ids_ref[...].astype(F32)) * CAP + column(pos_ref[...])
    gate = column(gate_ref[...].astype(F32))
    back = back_ref[...]
    part = routes // 4
    grads = []
    for p in range(4):
        here = slice(p * part, (p + 1) * part)
        onehot = (iota((part, slots), 1).astype(F32) == slot[here]).astype(F32).astype(BF16)
        rows = dot(onehot, back)
        out_ref[here, :] = (rows * gate[here]).astype(BF16)
        grads.append(jnp.sum(rows * hidden_ref[here, :].astype(F32), axis=1, keepdims=True))
    grad = jnp.where(own, jnp.concatenate(grads, axis=0), 0.0).astype(BF16)
    gate_out_ref[...] = lax.dot_general(
        grad, spread, (((0,), (0,)), ((), ())), preferred_element_type=F32
    ).astype(BF16)


def finish_kernel(*refs):
    out_ref = refs[-1]
    half = out_ref.shape[1] // 2
    for h in range(2):
        parts = refs[h * SIDE : (h + 1) * SIDE]
        for e in range(half):
            total = sum(p[e].astype(F32) for p in parts)
            out_ref[:, h * half + e, :] = total.T


def shift(x, axis, step):
    pairs = []
    for i in range(SIDE):
        for j in range(SIDE):
            to = ((i + step) % SIDE, j) if axis == 0 else (i, (j + step) % SIDE)
            pairs.append((i * SIDE + j, to[0] * SIDE + to[1]))
    return lax.ppermute(x, "dp", pairs)


def gather_half(weights, first):
    second = 1 - first
    blocks = [weights] + [shift(weights, first, -d) for d in range(1, SIDE)]
    b0 = jnp.stack([b[0] for b in blocks])
    b1 = jnp.stack([b[1] for b in blocks])
    right_1 = shift(b0, second, 1)
    left_1 = shift(b1, second, -1)
    right_2 = shift(b1, second, 1)
    left_2 = shift(b0, second, -1)
    right_3 = shift(right_1, second, 1)
    left_3 = shift(left_1, second, -1)
    return [[b0, left_2, right_3, right_1], [b1, left_1, left_3, right_2]]


def add(*parts):
    return sum(p.astype(F32) for p in parts)


def scatter_half(messages, first):
    second = 1 - first
    m0, m1 = messages
    right_1 = shift(m0[2], first, 1)
    left_1 = shift(m1[2], first, -1)
    right_2 = shift(m1[1], first, 1)
    left_2 = shift(m0[3], first, -1)
    right_3 = shift(add(m0[1], right_1).astype(BF16), first, 1)
    left_3 = shift(add(m1[3], left_1).astype(BF16), first, -1)
    sums = [
        jnp.stack([add(m0[0][d], left_2[d], right_3[d]), add(m1[0][d], right_2[d], left_3[d])]).astype(BF16)
        for d in range(SIDE)
    ]
    return [sums[0]] + [shift(sums[d], second, d) for d in range(1, SIDE)]


VMEM = pl.BlockSpec(memory_space=pltpu.VMEM)
SMEM = pl.BlockSpec(memory_space=pltpu.SMEM)
ANY = pl.BlockSpec(memory_space=pl.ANY)


def params(mib):
    return pltpu.CompilerParams(vmem_limit_bytes=mib * 2**20)


def cost(flops, moved):
    return pl.CostEstimate(flops=int(flops), bytes_accessed=int(moved), transcendentals=0)


def sds(shape, dtype):
    return jax.ShapeDtypeStruct(shape, dtype)


def pack(owners, local, ids, gate, hidden):
    routes, width = hidden.shape
    return pl.pallas_call(
        functools.partial(pack_kernel, owners, local),
        out_shape=[sds((owners, local * CAP + EXTRA, width), BF16), sds(ids.shape, F32)],
        in_specs=[VMEM] * 3,
        out_specs=[VMEM] * 2,
        compiler_params=params(40),
        cost_estimate=cost(2 * owners * local * CAP * routes * width, 2**22),
        name="pack",
    )(ids, gate, hidden)


def grad_down_call(local, xy, wire, grads):
    owners, tokens, model = grads.shape
    width = wire.shape[2]
    rows = owners * CAP
    return pl.pallas_call(
        functools.partial(grad_down_kernel, local),
        out_shape=[sds((SIDE, width, 128), BF16)] * (local * SIDE) + [sds((local, rows, model), BF16)],
        in_specs=[SMEM, VMEM, ANY],
        out_specs=[ANY] * (local * SIDE + 1),
        scratch_shapes=[
            pltpu.VMEM((owners, tokens, model), BF16),
            pltpu.VMEM((local, rows, model), BF16),
            pltpu.VMEM((local, width, model), BF16),
            pltpu.SemaphoreType.DMA((owners // 2,)),
            pltpu.SemaphoreType.DMA((local,)),
            pltpu.SemaphoreType.DMA((local, SIDE, SIDE)),
        ],
        compiler_params=params(48),
        cost_estimate=cost(4e9, 22e6),
        name="grad_down",
    )(xy, wire, grads)


def hidden_call(local, xy, x, pieces):
    _, rows, model = x.shape
    depth, width = pieces[0].shape[1:]
    owners = rows // CAP
    return pl.pallas_call(
        functools.partial(hidden_kernel, local),
        out_shape=sds((owners, local * CAP, width), BF16),
        in_specs=[SMEM] + [ANY] * (1 + len(pieces)),
        out_specs=VMEM,
        scratch_shapes=[
            pltpu.VMEM((local, rows, model), BF16),
            pltpu.VMEM((local, model, width), BF16),
            pltpu.VMEM((owners, local * CAP, width), F32),
            pltpu.SemaphoreType.DMA((local,)),
            pltpu.SemaphoreType.DMA((local, SIDE, SIDE)),
        ],
        compiler_params=params(48),
        cost_estimate=cost(2.4e9, 14e6),
        name="hidden_grad",
    )(xy, x, *pieces)


def unpack(ids, pos, gate, hidden, back):
    routes, width = hidden.shape
    return pl.pallas_call(
        unpack_kernel,
        out_shape=[sds((routes, width), BF16), sds(ids.shape, BF16)],
        in_specs=[VMEM] * 5,
        out_specs=[VMEM] * 2,
        compiler_params=params(40),
        cost_estimate=cost(2 * back.shape[0] * routes * width, 2**22),
        name="unpack",
    )(ids, pos, gate, hidden, back)


def finish(parts, depth, local, width):
    return pl.pallas_call(
        finish_kernel,
        out_shape=sds((depth, local, width), F32),
        in_specs=[VMEM] * len(parts),
        out_specs=VMEM,
        compiler_params=params(32),
        cost_estimate=cost(2**20, 2.5e6),
        name="finish",
    )(*parts)


def per_device(out_grad, saved_hidden, gate_weight, expert_ids, down_weight):
    tokens, top = expert_ids.shape
    model = out_grad.shape[1]
    width = saved_hidden.shape[2]
    owners = lax.axis_size("expert")
    depth, local, _ = down_weight.shape
    at = lax.axis_index("dp").astype(I32)
    xy = jnp.stack([at // SIDE, at % SIDE])

    grads = lax.all_gather(out_grad, "expert", axis=0, tiled=True).reshape(owners, tokens, model)
    weights = down_weight.transpose(1, 0, 2)
    ids, gate = expert_ids.T, gate_weight.T
    hidden = saved_hidden.reshape(tokens * top, width)
    wire, pos = pack(owners, local, ids, gate, hidden)
    wire = lax.all_to_all(wire, "expert", split_axis=0, concat_axis=0, tiled=True)

    halves = (gather_half(weights[: local // 2], 0), gather_half(weights[local // 2 :], 1))
    pieces = [p for half in halves for one in half for p in one]

    *messages, x = grad_down_call(local, xy, wire, grads)
    messages = [messages[e * SIDE : (e + 1) * SIDE] for e in range(local)]
    sums = scatter_half(messages[: local // 2], 0) + scatter_half(messages[local // 2 :], 1)

    u = hidden_call(local, xy, x, pieces)
    back = lax.all_to_all(u, "expert", split_axis=0, concat_axis=0, tiled=True)
    back = back.reshape(owners * local * CAP, width)
    grad_hidden, grad_gate = unpack(ids, pos, gate, hidden, back)
    grad_down = finish(sums, depth, local, width)
    return grad_hidden.reshape(tokens, top, width), grad_gate.T, grad_down


def solution(mesh):
    in_specs = (
        P(("dp", "expert"), None),
        P(("dp", "expert"), None, None),
        P(("dp", "expert"), None),
        P(("dp", "expert"), None),
        P("dp", "expert", None),
    )
    out_specs = (
        P(("dp", "expert"), None, None),
        P(("dp", "expert"), None),
        P("dp", "expert", None),
    )
    return jax.shard_map(
        per_device, mesh=mesh, in_specs=in_specs, out_specs=out_specs, check_vma=False
    )
```

```python
import functools

import jax
import jax.numpy as jnp
from jax import lax
from jax.experimental import pallas as pl
from jax.experimental.pallas import tpu as pltpu
from jax.sharding import PartitionSpec as P

CAP = 24
SIDE = 4
EXTRA = 8
BF16, F32, I32 = jnp.bfloat16, jnp.float32, jnp.int32


def iota(shape, dim):
    return lax.broadcasted_iota(I32, shape, dim)


def dot(a, b):
    return jnp.dot(a, b, preferred_element_type=F32)


def pack_kernel(owners, local, ids_ref, gate_ref, hidden_ref, wire_ref, pos_ref):
    top, tokens = ids_ref.shape
    routes, width = hidden_ref.shape
    experts = owners * local
    ids = ids_ref[...]
    expert_no = iota((experts, tokens), 0)
    named = [expert_no == ids[k : k + 1, :] for k in range(top)]
    member = sum(n.astype(F32) for n in named)
    earlier = (iota((tokens, tokens), 0) < iota((tokens, tokens), 1)).astype(F32).astype(BF16)
    before = dot(member.astype(BF16), earlier)
    pos = jnp.concatenate(
        [jnp.sum(jnp.where(n, before, 0.0), axis=0, keepdims=True) for n in named], axis=0
    )
    pos_ref[...] = pos
    spread = (iota((tokens, routes), 1) // top == iota((tokens, routes), 0)).astype(F32).astype(BF16)
    own = iota((top, routes), 1) % top == iota((top, routes), 0)

    def row(x):
        return jnp.sum(jnp.where(own, dot(x.astype(BF16), spread), 0.0), axis=0, keepdims=True)

    slot_row = row(ids.astype(F32)) * CAP + row(pos)
    gate_row = row(gate_ref[...].astype(F32))
    slots = jnp.where(member > 0.0, before, -1.0).astype(BF16)
    r, c = iota((owners * EXTRA, experts), 0), iota((owners * EXTRA, experts), 1)
    pick = ((r % EXTRA < local) & (c == r // EXTRA * local + r % EXTRA)).astype(F32).astype(BF16)
    slots = dot(pick, slots)
    slots = jnp.concatenate([slots, jnp.zeros((owners * EXTRA, width - tokens), F32)], axis=1)
    rows = local * CAP
    group = 4
    hidden = hidden_ref[...]
    for g in range(owners // group):
        row_no = (iota((group * rows, routes), 0) + g * group * rows).astype(F32)
        onehot = jnp.where(row_no == slot_row, gate_row, 0.0).astype(BF16)
        packed = dot(onehot, hidden)
        for i in range(group):
            o = g * group + i
            wire_ref[o] = jnp.concatenate(
                [packed[i * rows : (i + 1) * rows], slots[o * EXTRA : (o + 1) * EXTRA]], axis=0
            ).astype(BF16)


def place(first_is_x, a, b, at_ref):
    dx, dy = (a, b) if first_is_x else (b, a)
    x, y = (at_ref[0] + dx) % SIDE, (at_ref[1] + dy) % SIDE
    return x * SIDE + y


def expert_kernel(local, steps, at_ref, wire_ref, weight_hbm, *refs):
    pieces, refs = refs[: len(steps)], refs[len(steps) :]
    messages, u_ref = refs[: local * SIDE], refs[local * SIDE]
    gbuf, xbuf, abuf, wbuf, ubuf, gsem, wsem, msem = refs[local * SIDE + 1 :]
    owners, tokens, model = gbuf.shape
    width = wire_ref.shape[2]
    chips = owners // 2
    loads = []
    for n, (dz, lane, start) in enumerate(steps):
        source = (at_ref[2] + dz) % chips * 2 + (at_ref[3] + lane) % 2
        rows = pieces[n].shape[0]
        loads.append(
            pltpu.make_async_copy(pieces[n], gbuf.at[source, pl.ds(start, rows)], gsem.at[n])
        )
        loads[-1].start()
    weights = [
        pltpu.make_async_copy(weight_hbm.at[:, e], wbuf.at[e], wsem.at[e]) for e in range(local)
    ]
    for c in weights:
        c.start()
    wire = wire_ref[...].astype(F32)
    block = 2 * CAP
    for c in loads:
        c.wait()
    for p in range(chips):
        slot = [wire[2 * p + i, local * CAP : local * CAP + EXTRA, :tokens] for i in range(2)]
        slot[1] = jnp.where(slot[1] >= 0.0, slot[1] + CAP, -1.0)
        slot = jnp.concatenate(slot, axis=1)
        onehot = jnp.concatenate(
            [
                (slot[e : e + 1, :] == iota((block, 2 * tokens), 0).astype(F32)).astype(F32)
                for e in range(local)
            ],
            axis=0,
        ).astype(BF16)
        rows = dot(onehot, gbuf[2 * p : 2 * p + 2].reshape(2 * tokens, model)).astype(BF16)
        for e in range(local):
            xbuf[e, p * block : (p + 1) * block, :] = rows[e * block : (e + 1) * block]
    copies = []
    for e in range(local):
        hidden = wire[:, e * CAP : (e + 1) * CAP, :].reshape(owners * CAP, width)
        hidden = hidden.T.astype(BF16)
        step = model // 4
        for n in range(4):
            here = slice(n * step, (n + 1) * step)
            abuf[e, :, here] = dot(hidden, xbuf[e, :, here]).astype(BF16)
        for a in range(SIDE):
            for b in range(SIDE):
                at = pl.multiple_of(place(e < local // 2, a, b, at_ref) * 128, 128)
                copies.append(
                    pltpu.make_async_copy(
                        abuf.at[e, :, pl.ds(at, 128)], messages[e * SIDE + a].at[b], msem.at[e, a, b]
                    )
                )
                copies[-1].start()
    for e in range(local):
        weights[e].wait()
        u = dot(xbuf[e], wbuf[e].reshape(model, width))
        ubuf[:, e * CAP : (e + 1) * CAP, :] = u.reshape(owners, CAP, width)
    u_ref[...] = ubuf[...].astype(BF16)
    for c in copies:
        c.wait()


def unpack_kernel(ids_ref, pos_ref, gate_ref, hidden_ref, back_ref, out_ref, gate_out_ref):
    top, tokens = ids_ref.shape
    routes, width = hidden_ref.shape
    slots = back_ref.shape[0]
    spread = (iota((routes, tokens), 0) // top == iota((routes, tokens), 1)).astype(F32).astype(BF16)
    own = iota((routes, top), 0) % top == iota((routes, top), 1)

    def column(x):
        y = lax.dot_general(spread, x.astype(BF16), (((1,), (1,)), ((), ())), preferred_element_type=F32)
        return jnp.sum(jnp.where(own, y, 0.0), axis=1, keepdims=True)

    slot = column(ids_ref[...].astype(F32)) * CAP + column(pos_ref[...])
    gate = column(gate_ref[...].astype(F32))
    back = back_ref[...]
    part = routes // 4
    grads = []
    for p in range(4):
        here = slice(p * part, (p + 1) * part)
        onehot = (iota((part, slots), 1).astype(F32) == slot[here]).astype(F32).astype(BF16)
        rows = dot(onehot, back)
        out_ref[here, :] = (rows * gate[here]).astype(BF16)
        grads.append(jnp.sum(rows * hidden_ref[here, :].astype(F32), axis=1, keepdims=True))
    grad = jnp.where(own, jnp.concatenate(grads, axis=0), 0.0).astype(BF16)
    gate_out_ref[...] = lax.dot_general(
        grad, spread, (((0,), (0,)), ((), ())), preferred_element_type=F32
    ).astype(BF16)


def finish_kernel(*refs):
    out_ref = refs[-1]
    half = out_ref.shape[1] // 2
    for h in range(2):
        parts = refs[h * SIDE : (h + 1) * SIDE]
        for e in range(half):
            total = sum(p[e].astype(F32) for p in parts)
            out_ref[:, h * half + e, :] = total.T


def shift(x, axis, step):
    pairs = []
    for i in range(SIDE):
        for j in range(SIDE):
            to = ((i + step) % SIDE, j) if axis == 0 else (i, (j + step) % SIDE)
            pairs.append((i * SIDE + j, to[0] * SIDE + to[1]))
    return lax.ppermute(x, "dp", pairs)


def shift_expert(x, step, swap=False):
    n = lax.axis_size("expert")
    pairs = [(i, i ^ 1 if swap else (i + 2 * step) % n) for i in range(n)]
    return lax.ppermute(x, "expert", pairs)


def ring_gather(x):
    chips = lax.axis_size("expert") // 2
    half = x.shape[0] // 2
    got = [(x, 0, 0)]
    right = left = x
    for d in range(1, chips // 2):
        right, left = shift_expert(right, 1), shift_expert(left, -1)
        got += [(right, chips - d, 0), (left, d, 0)]
    got.append((shift_expert(right[:half], 1), chips // 2, 0))
    got.append((shift_expert(left[half:], -1), chips // 2, half))
    pieces = [p for p, _, _ in got] + [shift_expert(p, 0, True) for p, _, _ in got]
    steps = [(d, lane, start) for lane in range(2) for _, d, start in got]
    return pieces, steps


def add(*parts):
    return sum(p.astype(F32) for p in parts)


def scatter_half(messages, first):
    second = 1 - first
    m0, m1 = messages
    right_1 = shift(m0[2], first, 1)
    left_1 = shift(m1[2], first, -1)
    right_2 = shift(m1[1], first, 1)
    left_2 = shift(m0[3], first, -1)
    right_3 = shift(add(m0[1], right_1).astype(BF16), first, 1)
    left_3 = shift(add(m1[3], left_1).astype(BF16), first, -1)
    sums = [
        jnp.stack([add(m0[0][d], left_2[d], right_3[d]), add(m1[0][d], right_2[d], left_3[d])]).astype(BF16)
        for d in range(SIDE)
    ]
    return [sums[0]] + [shift(sums[d], second, d) for d in range(1, SIDE)]


VMEM = pl.BlockSpec(memory_space=pltpu.VMEM)
SMEM = pl.BlockSpec(memory_space=pltpu.SMEM)
ANY = pl.BlockSpec(memory_space=pl.ANY)


def params(mib):
    return pltpu.CompilerParams(vmem_limit_bytes=mib * 2**20)


def cost(flops, moved):
    return pl.CostEstimate(flops=int(flops), bytes_accessed=int(moved), transcendentals=0)


def sds(shape, dtype):
    return jax.ShapeDtypeStruct(shape, dtype)


def pack(owners, local, ids, gate, hidden):
    routes, width = hidden.shape
    return pl.pallas_call(
        functools.partial(pack_kernel, owners, local),
        out_shape=[sds((owners, local * CAP + EXTRA, width), BF16), sds(ids.shape, F32)],
        in_specs=[VMEM] * 3,
        out_specs=[VMEM] * 2,
        compiler_params=params(20),
        cost_estimate=cost(2 * owners * local * CAP * routes * width, 2**22),
        name="pack",
    )(ids, gate, hidden)


def expert_call(local, at, wire, weights, pieces, steps):
    tokens, model = pieces[0].shape
    owners, _, width = wire.shape
    rows = owners * CAP
    return pl.pallas_call(
        functools.partial(expert_kernel, local, steps),
        out_shape=[sds((SIDE, width, 128), BF16)] * (local * SIDE)
        + [sds((owners, local * CAP, width), BF16)],
        in_specs=[SMEM, VMEM, ANY] + [ANY] * len(pieces),
        out_specs=[ANY] * (local * SIDE) + [VMEM],
        scratch_shapes=[
            pltpu.VMEM((owners, tokens, model), BF16),
            pltpu.VMEM((local, rows, model), BF16),
            pltpu.VMEM((local, width, model), BF16),
            pltpu.VMEM((local, SIDE * SIDE, model // SIDE // SIDE, width), BF16),
            pltpu.VMEM((owners, local * CAP, width), F32),
            pltpu.SemaphoreType.DMA((len(pieces),)),
            pltpu.SemaphoreType.DMA((local,)),
            pltpu.SemaphoreType.DMA((local, SIDE, SIDE)),
        ],
        compiler_params=params(44),
        cost_estimate=cost(6.4e9, 24e6),
        name="experts",
    )(at, wire, weights, *pieces)


def unpack(ids, pos, gate, hidden, back):
    routes, width = hidden.shape
    return pl.pallas_call(
        unpack_kernel,
        out_shape=[sds((routes, width), BF16), sds(ids.shape, BF16)],
        in_specs=[VMEM] * 5,
        out_specs=[VMEM] * 2,
        compiler_params=params(20),
        cost_estimate=cost(2 * back.shape[0] * routes * width, 2**22),
        name="unpack",
    )(ids, pos, gate, hidden, back)


def finish(parts, depth, local, width):
    return pl.pallas_call(
        finish_kernel,
        out_shape=sds((depth, local, width), F32),
        in_specs=[VMEM] * len(parts),
        out_specs=VMEM,
        compiler_params=params(12),
        cost_estimate=cost(2**20, 2.5e6),
        name="finish",
    )(*parts)


def per_device(out_grad, saved_hidden, gate_weight, expert_ids, down_weight):
    tokens, top = expert_ids.shape
    width = saved_hidden.shape[2]
    owners = lax.axis_size("expert")
    depth, local, _ = down_weight.shape
    dp, own = lax.axis_index("dp").astype(I32), lax.axis_index("expert").astype(I32)
    at = jnp.stack([dp // SIDE, dp % SIDE, own // 2, own % 2])

    weights = lax.all_gather(down_weight.transpose(1, 0, 2), "dp", axis=0, tiled=False)
    pieces, steps = ring_gather(out_grad)
    ids, gate = expert_ids.T, gate_weight.T
    hidden = saved_hidden.reshape(tokens * top, width)
    wire, pos = pack(owners, local, ids, gate, hidden)
    wire = lax.all_to_all(wire, "expert", split_axis=0, concat_axis=0, tiled=True)

    *messages, u = expert_call(local, at, wire, weights, pieces, steps)
    messages = [messages[e * SIDE : (e + 1) * SIDE] for e in range(local)]
    sums = scatter_half(messages[: local // 2], 0) + scatter_half(messages[local // 2 :], 1)
    back = lax.all_to_all(u, "expert", split_axis=0, concat_axis=0, tiled=True)
    back = back.reshape(owners * local * CAP, width)
    grad_hidden, grad_gate = unpack(ids, pos, gate, hidden, back)
    grad_down = finish(sums, depth, local, width)
    return grad_hidden.reshape(tokens, top, width), grad_gate.T, grad_down


def solution(mesh):
    in_specs = (
        P(("dp", "expert"), None),
        P(("dp", "expert"), None, None),
        P(("dp", "expert"), None),
        P(("dp", "expert"), None),
        P("dp", "expert", None),
    )
    out_specs = (
        P(("dp", "expert"), None, None),
        P(("dp", "expert"), None),
        P("dp", "expert", None),
    )
    return jax.shard_map(
        per_device, mesh=mesh, in_specs=in_specs, out_specs=out_specs, check_vma=False
    )
```

```python
import functools

import jax
import jax.numpy as jnp
from jax import lax
from jax.experimental import pallas as pl
from jax.experimental.pallas import tpu as pltpu
from jax.sharding import PartitionSpec as P

CAP = 24
SIDE = 4
EXTRA = 8
BF16, F32, I32 = jnp.bfloat16, jnp.float32, jnp.int32


def iota(shape, dim):
    return lax.broadcasted_iota(I32, shape, dim)


def dot(a, b):
    return jnp.dot(a, b, preferred_element_type=F32)


def pack_kernel(owners, local, ids_ref, gate_ref, hidden_ref, wire_ref, pos_ref):
    top, tokens = ids_ref.shape
    routes, width = hidden_ref.shape
    experts = owners * local
    ids = ids_ref[...]
    expert_no = iota((experts, tokens), 0)
    named = [expert_no == ids[k : k + 1, :] for k in range(top)]
    member = sum(n.astype(F32) for n in named)
    earlier = (iota((tokens, tokens), 0) < iota((tokens, tokens), 1)).astype(F32).astype(BF16)
    before = dot(member.astype(BF16), earlier)
    pos = jnp.concatenate(
        [jnp.sum(jnp.where(n, before, 0.0), axis=0, keepdims=True) for n in named], axis=0
    )
    pos_ref[...] = pos
    spread = (iota((tokens, routes), 1) // top == iota((tokens, routes), 0)).astype(F32).astype(BF16)
    own = iota((top, routes), 1) % top == iota((top, routes), 0)

    def row(x):
        return jnp.sum(jnp.where(own, dot(x.astype(BF16), spread), 0.0), axis=0, keepdims=True)

    slot_row = row(ids.astype(F32)) * CAP + row(pos)
    gate_row = row(gate_ref[...].astype(F32))
    slots = jnp.where(member > 0.0, before, -1.0).astype(BF16)
    r, c = iota((owners * EXTRA, experts), 0), iota((owners * EXTRA, experts), 1)
    pick = ((r % EXTRA < local) & (c == r // EXTRA * local + r % EXTRA)).astype(F32).astype(BF16)
    slots = dot(pick, slots)
    slots = jnp.concatenate([slots, jnp.zeros((owners * EXTRA, width - tokens), F32)], axis=1)
    rows = local * CAP
    group = 4
    hidden = hidden_ref[...]
    for g in range(owners // group):
        row_no = (iota((group * rows, routes), 0) + g * group * rows).astype(F32)
        onehot = jnp.where(row_no == slot_row, gate_row, 0.0).astype(BF16)
        packed = dot(onehot, hidden)
        for i in range(group):
            o = g * group + i
            wire_ref[o] = jnp.concatenate(
                [packed[i * rows : (i + 1) * rows], slots[o * EXTRA : (o + 1) * EXTRA]], axis=0
            ).astype(BF16)


def expert_kernel(local, at_ref, wire_ref, grad_hbm, *refs):
    half = local // 2
    pieces, refs = refs[: 2 * SIDE], refs[2 * SIDE :]
    messages, u_hbm = refs[: 2 * SIDE], refs[2 * SIDE]
    gbuf, xbuf, abuf, wbuf, ubuf, obuf, gsem, wsem, msem, usem = refs[2 * SIDE + 1 :]
    owners, tokens, model = gbuf.shape
    width = wire_ref.shape[2]
    depth = model // (SIDE * SIDE)
    chips = owners // 2
    loads = [
        pltpu.make_async_copy(grad_hbm.at[pl.ds(2 * p, 2)], gbuf.at[pl.ds(2 * p, 2)], gsem.at[p])
        for p in range(chips)
    ]
    weights = [
        [pltpu.make_async_copy(pieces[h * SIDE + a], wbuf.at[h, a], wsem.at[h, a]) for a in range(SIDE)]
        for h in range(2)
    ]
    for c in loads + weights[0] + weights[1]:
        c.start()
    places = []
    for d in range(SIDE * SIDE):
        dx = (d // SIDE + SIDE - at_ref[0]) % SIDE
        dy = (d % SIDE + SIDE - at_ref[1]) % SIDE
        places.append(pl.multiple_of((dx * SIDE + dy) * depth, depth))
    block = 2 * CAP
    for p in range(chips):
        slot = [
            wire_ref[2 * p + i, local * CAP : local * CAP + EXTRA, :tokens].astype(F32)
            for i in range(2)
        ]
        slot[1] = jnp.where(slot[1] >= 0.0, slot[1] + CAP, -1.0)
        slot = jnp.concatenate(slot, axis=1)
        onehot = jnp.concatenate(
            [
                (slot[e : e + 1, :] == iota((block, 2 * tokens), 0).astype(F32)).astype(F32)
                for e in range(local)
            ],
            axis=0,
        ).astype(BF16)
        loads[p].wait()
        rows = dot(onehot, gbuf[2 * p : 2 * p + 2].reshape(2 * tokens, model)).astype(BF16)
        for e in range(local):
            for d in range(SIDE * SIDE):
                xbuf[e, p * block : (p + 1) * block, pl.ds(places[d], depth)] = rows[
                    e * block : (e + 1) * block, d * depth : (d + 1) * depth
                ]
    copies = []
    wire = wire_ref[:, : local * CAP, :].astype(F32)
    step = SIDE * depth
    for e in range(local):
        hidden = wire[:, e * CAP : (e + 1) * CAP, :].reshape(owners * CAP, width)
        hidden = hidden.T.astype(BF16)
        h = e // half
        for dx in range(SIDE):
            grad = dot(hidden, xbuf[e, :, dx * step : (dx + 1) * step]).astype(BF16)
            for dy in range(SIDE):
                a, b = (dx, dy) if h == 0 else (dy, dx)
                abuf[h, a, b, e % half] = grad[:, dy * depth : (dy + 1) * depth]
        if e % half == half - 1:
            for a in range(SIDE):
                copies.append(
                    pltpu.make_async_copy(abuf.at[h, a], messages[h * SIDE + a], msem.at[h, a])
                )
                copies[-1].start()
    for e in range(local):
        h = e // half
        if e % half == 0:
            for c in weights[h]:
                c.wait()
        u = jnp.zeros((owners * CAP, width), F32)
        for dx in range(SIDE):
            w = wbuf[0, :, dx, e % half] if h == 0 else wbuf[1, dx, :, e % half]
            u += dot(xbuf[e, :, dx * step : (dx + 1) * step], w.reshape(step, width))
        ubuf[:, e * CAP : (e + 1) * CAP, :] = u.reshape(owners, CAP, width)
    obuf[...] = ubuf[...].astype(BF16)
    copies.append(pltpu.make_async_copy(obuf, u_hbm, usem))
    copies[-1].start()
    for c in copies:
        c.wait()


def unpack_kernel(ids_ref, pos_ref, gate_ref, hidden_ref, back_ref, out_ref, gate_out_ref):
    top, tokens = ids_ref.shape
    routes, width = hidden_ref.shape
    slots = back_ref.shape[0]
    spread = (iota((routes, tokens), 0) // top == iota((routes, tokens), 1)).astype(F32).astype(BF16)
    own = iota((routes, top), 0) % top == iota((routes, top), 1)

    def column(x):
        y = lax.dot_general(spread, x.astype(BF16), (((1,), (1,)), ((), ())), preferred_element_type=F32)
        return jnp.sum(jnp.where(own, y, 0.0), axis=1, keepdims=True)

    slot = column(ids_ref[...].astype(F32)) * CAP + column(pos_ref[...])
    gate = column(gate_ref[...].astype(F32))
    back = back_ref[...]
    part = routes // 4
    grads = []
    for p in range(4):
        here = slice(p * part, (p + 1) * part)
        onehot = (iota((part, slots), 1).astype(F32) == slot[here]).astype(F32).astype(BF16)
        rows = dot(onehot, back)
        out_ref[here, :] = (rows * gate[here]).astype(BF16)
        grads.append(jnp.sum(rows * hidden_ref[here, :].astype(F32), axis=1, keepdims=True))
    grad = jnp.where(own, jnp.concatenate(grads, axis=0), 0.0).astype(BF16)
    gate_out_ref[...] = lax.dot_general(
        grad, spread, (((0,), (0,)), ((), ())), preferred_element_type=F32
    ).astype(BF16)


def finish_kernel(*refs):
    out_ref = refs[-1]
    half = out_ref.shape[1] // 2
    for h in range(2):
        parts = refs[h * SIDE : (h + 1) * SIDE]
        for e in range(half):
            total = sum(p[e].astype(F32) for p in parts)
            out_ref[:, h * half + e, :] = total.T


def shift(x, axis, step):
    pairs = []
    for i in range(SIDE):
        for j in range(SIDE):
            to = ((i + step) % SIDE, j) if axis == 0 else (i, (j + step) % SIDE)
            pairs.append((i * SIDE + j, to[0] * SIDE + to[1]))
    return lax.ppermute(x, "dp", pairs)


def gather_half(weights, first):
    blocks = jnp.stack([weights] + [shift(weights, first, -d) for d in range(1, SIDE)])
    return [blocks] + [shift(blocks, 1 - first, -d) for d in range(1, SIDE)]


def add(*parts):
    return sum(p.astype(F32) for p in parts)


def scatter_half(messages, first):
    got = [messages[0]] + [shift(messages[d], first, d) for d in range(1, SIDE)]
    sums = [add(*[g[d] for g in got]).astype(BF16) for d in range(SIDE)]
    return [sums[0]] + [shift(sums[d], 1 - first, d) for d in range(1, SIDE)]


VMEM = pl.BlockSpec(memory_space=pltpu.VMEM)
SMEM = pl.BlockSpec(memory_space=pltpu.SMEM)
ANY = pl.BlockSpec(memory_space=pl.ANY)
HBM = pl.BlockSpec(memory_space=pltpu.HBM)


def params(mib):
    return pltpu.CompilerParams(vmem_limit_bytes=mib * 2**20)


def cost(flops, moved):
    return pl.CostEstimate(flops=int(flops), bytes_accessed=int(moved), transcendentals=0)


def sds(shape, dtype):
    return jax.ShapeDtypeStruct(shape, dtype)


def pack(owners, local, ids, gate, hidden):
    routes, width = hidden.shape
    return pl.pallas_call(
        functools.partial(pack_kernel, owners, local),
        out_shape=[sds((owners, local * CAP + EXTRA, width), BF16), sds(ids.shape, F32)],
        in_specs=[VMEM] * 3,
        out_specs=[VMEM] * 2,
        compiler_params=params(20),
        cost_estimate=cost(2 * owners * local * CAP * routes * width, 2**22),
        name="pack",
    )(ids, gate, hidden)


def expert_call(local, at, wire, grads, pieces):
    owners, tokens, model = grads.shape
    width = wire.shape[2]
    depth = model // (SIDE * SIDE)
    rows = owners * CAP
    return pl.pallas_call(
        functools.partial(expert_kernel, local),
        out_shape=[sds((SIDE, local // 2, width, depth), BF16)] * (2 * SIDE)
        + [sds((owners, local * CAP, width), BF16)],
        in_specs=[SMEM, VMEM] + [HBM] * (1 + len(pieces)),
        out_specs=[HBM] * (2 * SIDE + 1),
        scratch_shapes=[
            pltpu.VMEM((owners, tokens, model), BF16),
            pltpu.VMEM((local, rows, model), BF16),
            pltpu.VMEM((2, SIDE, SIDE, local // 2, width, depth), BF16),
            pltpu.VMEM((2, SIDE, SIDE, local // 2, depth, width), BF16),
            pltpu.VMEM((owners, local * CAP, width), F32),
            pltpu.VMEM((owners, local * CAP, width), BF16),
            pltpu.SemaphoreType.DMA((owners // 2,)),
            pltpu.SemaphoreType.DMA((2, SIDE)),
            pltpu.SemaphoreType.DMA((2, SIDE)),
            pltpu.SemaphoreType.DMA,
        ],
        compiler_params=params(40),
        cost_estimate=cost(6.4e9, 24e6),
        name="experts",
    )(at, wire, grads, *pieces)


def unpack(ids, pos, gate, hidden, back):
    routes, width = hidden.shape
    return pl.pallas_call(
        unpack_kernel,
        out_shape=[sds((routes, width), BF16), sds(ids.shape, BF16)],
        in_specs=[VMEM] * 5,
        out_specs=[VMEM] * 2,
        compiler_params=params(20),
        cost_estimate=cost(2 * back.shape[0] * routes * width, 2**22),
        name="unpack",
    )(ids, pos, gate, hidden, back)


def finish(parts, depth, local, width):
    return pl.pallas_call(
        finish_kernel,
        out_shape=sds((depth, local, width), F32),
        in_specs=[VMEM] * len(parts),
        out_specs=VMEM,
        compiler_params=params(12),
        cost_estimate=cost(2**20, 2.5e6),
        name="finish",
    )(*parts)


def per_device(out_grad, saved_hidden, gate_weight, expert_ids, down_weight):
    tokens, top = expert_ids.shape
    width = saved_hidden.shape[2]
    owners = lax.axis_size("expert")
    depth, local, _ = down_weight.shape
    dp = lax.axis_index("dp").astype(I32)
    at = jnp.stack([dp // SIDE, dp % SIDE])
    half = local // 2

    grads = lax.all_gather(out_grad, "expert", axis=0, tiled=False)
    ids, gate = expert_ids.T, gate_weight.T
    hidden = saved_hidden.reshape(tokens * top, width)
    wire, pos = pack(owners, local, ids, gate, hidden)
    wire = lax.all_to_all(wire, "expert", split_axis=0, concat_axis=0, tiled=True)
    weights = down_weight.transpose(1, 0, 2)
    pieces = gather_half(weights[:half], 0) + gather_half(weights[half:], 1)

    *messages, u = expert_call(local, at, wire, grads, pieces)
    back = lax.all_to_all(u, "expert", split_axis=0, concat_axis=0, tiled=True)
    sums = scatter_half(messages[:SIDE], 0) + scatter_half(messages[SIDE:], 1)
    back = back.reshape(owners * local * CAP, width)
    grad_hidden, grad_gate = unpack(ids, pos, gate, hidden, back)
    grad_down = finish(sums, depth, local, width)
    return grad_hidden.reshape(tokens, top, width), grad_gate.T, grad_down


def solution(mesh):
    in_specs = (
        P(("dp", "expert"), None),
        P(("dp", "expert"), None, None),
        P(("dp", "expert"), None),
        P(("dp", "expert"), None),
        P("dp", "expert", None),
    )
    out_specs = (
        P(("dp", "expert"), None, None),
        P(("dp", "expert"), None),
        P("dp", "expert", None),
    )
    return jax.shard_map(
        per_device, mesh=mesh, in_specs=in_specs, out_specs=out_specs, check_vma=False
    )
```

```python
import functools

import jax
import jax.numpy as jnp
from jax import lax
from jax.experimental import pallas as pl
from jax.experimental.pallas import tpu as pltpu
from jax.sharding import PartitionSpec as P

CAP = 24
SIDE = 4
EXTRA = 8
BF16, F32, I32 = jnp.bfloat16, jnp.float32, jnp.int32


def iota(shape, dim):
    return lax.broadcasted_iota(I32, shape, dim)


def dot(a, b):
    return jnp.dot(a, b, preferred_element_type=F32)


def pack_kernel(owners, local, ids_ref, gate_ref, hidden_ref, wire_ref, pos_ref):
    top, tokens = ids_ref.shape
    routes, width = hidden_ref.shape
    experts = owners * local
    ids = ids_ref[...]
    expert_no = iota((experts, tokens), 0)
    named = [expert_no == ids[k : k + 1, :] for k in range(top)]
    member = sum(n.astype(F32) for n in named)
    earlier = (iota((tokens, tokens), 0) < iota((tokens, tokens), 1)).astype(F32).astype(BF16)
    before = dot(member.astype(BF16), earlier)
    pos = jnp.concatenate(
        [jnp.sum(jnp.where(n, before, 0.0), axis=0, keepdims=True) for n in named], axis=0
    )
    pos_ref[...] = pos
    spread = (iota((tokens, routes), 1) // top == iota((tokens, routes), 0)).astype(F32).astype(BF16)
    own = iota((top, routes), 1) % top == iota((top, routes), 0)

    def row(x):
        return jnp.sum(jnp.where(own, dot(x.astype(BF16), spread), 0.0), axis=0, keepdims=True)

    slot_row = row(ids.astype(F32)) * CAP + row(pos)
    gate_row = row(gate_ref[...].astype(F32))
    slots = jnp.where(member > 0.0, before, -1.0).astype(BF16)
    r, c = iota((owners * EXTRA, experts), 0), iota((owners * EXTRA, experts), 1)
    pick = ((r % EXTRA < local) & (c == r // EXTRA * local + r % EXTRA)).astype(F32).astype(BF16)
    slots = dot(pick, slots)
    slots = jnp.concatenate([slots, jnp.zeros((owners * EXTRA, width - tokens), F32)], axis=1)
    rows = local * CAP
    group = 4
    hidden = hidden_ref[...]
    for g in range(owners // group):
        row_no = (iota((group * rows, routes), 0) + g * group * rows).astype(F32)
        onehot = jnp.where(row_no == slot_row, gate_row, 0.0).astype(BF16)
        packed = dot(onehot, hidden)
        for i in range(group):
            o = g * group + i
            wire_ref[o] = jnp.concatenate(
                [packed[i * rows : (i + 1) * rows], slots[o * EXTRA : (o + 1) * EXTRA]], axis=0
            ).astype(BF16)


def expert_kernel(local, at_ref, wire_ref, grad_hbm, *refs):
    half = local // 2
    pieces, refs = refs[: 2 * SIDE], refs[2 * SIDE :]
    messages, u_hbm = refs[: 2 * SIDE], refs[2 * SIDE]
    gbuf, xbuf, abuf, wbuf, ubuf, obuf, gsem, wsem, msem, usem = refs[2 * SIDE + 1 :]
    owners, tokens, model = gbuf.shape
    width = wire_ref.shape[2]
    depth = model // (SIDE * SIDE)
    chips = owners // 2
    loads = [
        pltpu.make_async_copy(grad_hbm.at[pl.ds(2 * p, 2)], gbuf.at[pl.ds(2 * p, 2)], gsem.at[p])
        for p in range(chips)
    ]
    weights = [
        [
            pltpu.make_async_copy(
                pieces[h * SIDE + k],
                wbuf.at[h, at_ref[2] * k + (1 - at_ref[2]) * ((SIDE - k) % SIDE)],
                wsem.at[h, k],
            )
            for k in range(SIDE)
        ]
        for h in range(2)
    ]
    for c in loads + weights[0] + weights[1]:
        c.start()
    places = []
    for d in range(SIDE * SIDE):
        dx = (d // SIDE + SIDE - at_ref[0]) % SIDE
        dy = (d % SIDE + SIDE - at_ref[1]) % SIDE
        places.append(pl.multiple_of((dx * SIDE + dy) * depth, depth))
    block = 2 * CAP
    for p in range(chips):
        slot = [
            wire_ref[2 * p + i, local * CAP : local * CAP + EXTRA, :tokens].astype(F32)
            for i in range(2)
        ]
        slot[1] = jnp.where(slot[1] >= 0.0, slot[1] + CAP, -1.0)
        slot = jnp.concatenate(slot, axis=1)
        onehot = jnp.concatenate(
            [
                (slot[e : e + 1, :] == iota((block, 2 * tokens), 0).astype(F32)).astype(F32)
                for e in range(local)
            ],
            axis=0,
        ).astype(BF16)
        loads[p].wait()
        rows = dot(onehot, gbuf[2 * p : 2 * p + 2].reshape(2 * tokens, model)).astype(BF16)
        for e in range(local):
            for d in range(SIDE * SIDE):
                xbuf[e, p * block : (p + 1) * block, pl.ds(places[d], depth)] = rows[
                    e * block : (e + 1) * block, d * depth : (d + 1) * depth
                ]
    copies = []
    wire = wire_ref[:, : local * CAP, :].astype(F32)
    step = SIDE * depth
    for e in range(local):
        hidden = wire[:, e * CAP : (e + 1) * CAP, :].reshape(owners * CAP, width)
        hidden = hidden.T.astype(BF16)
        h = e // half
        for dx in range(SIDE):
            grad = dot(hidden, xbuf[e, :, dx * step : (dx + 1) * step]).astype(BF16)
            for dy in range(SIDE):
                a, b = (dx, dy) if h == 0 else (dy, dx)
                abuf[h, a, b, e % half] = grad[:, dy * depth : (dy + 1) * depth]
        if e % half == half - 1:
            for a in range(SIDE):
                copies.append(
                    pltpu.make_async_copy(abuf.at[h, a], messages[h * SIDE + a], msem.at[h, a])
                )
                copies[-1].start()
    for e in range(local):
        h = e // half
        if e % half == 0:
            for c in weights[h]:
                c.wait()
        u = jnp.zeros((owners * CAP, width), F32)
        for dx in range(SIDE):
            w = wbuf[0, :, dx, e % half] if h == 0 else wbuf[1, dx, :, e % half]
            u += dot(xbuf[e, :, dx * step : (dx + 1) * step], w.reshape(step, width))
        ubuf[:, e * CAP : (e + 1) * CAP, :] = u.reshape(owners, CAP, width)
    obuf[...] = ubuf[...].astype(BF16)
    copies.append(pltpu.make_async_copy(obuf, u_hbm, usem))
    copies[-1].start()
    for c in copies:
        c.wait()


def unpack_kernel(ids_ref, pos_ref, gate_ref, hidden_ref, back_ref, out_ref, gate_out_ref):
    top, tokens = ids_ref.shape
    routes, width = hidden_ref.shape
    slots = back_ref.shape[0]
    spread = (iota((routes, tokens), 0) // top == iota((routes, tokens), 1)).astype(F32).astype(BF16)
    own = iota((routes, top), 0) % top == iota((routes, top), 1)

    def column(x):
        y = lax.dot_general(spread, x.astype(BF16), (((1,), (1,)), ((), ())), preferred_element_type=F32)
        return jnp.sum(jnp.where(own, y, 0.0), axis=1, keepdims=True)

    slot = column(ids_ref[...].astype(F32)) * CAP + column(pos_ref[...])
    gate = column(gate_ref[...].astype(F32))
    back = back_ref[...]
    part = routes // 4
    grads = []
    for p in range(4):
        here = slice(p * part, (p + 1) * part)
        onehot = (iota((part, slots), 1).astype(F32) == slot[here]).astype(F32).astype(BF16)
        rows = dot(onehot, back)
        out_ref[here, :] = (rows * gate[here]).astype(BF16)
        grads.append(jnp.sum(rows * hidden_ref[here, :].astype(F32), axis=1, keepdims=True))
    grad = jnp.where(own, jnp.concatenate(grads, axis=0), 0.0).astype(BF16)
    gate_out_ref[...] = lax.dot_general(
        grad, spread, (((0,), (0,)), ((), ())), preferred_element_type=F32
    ).astype(BF16)


def finish_kernel(after_ref, *refs):
    out_ref = refs[-1]
    half = out_ref.shape[1] // 2
    for h in range(2):
        parts = refs[h * SIDE : (h + 1) * SIDE]
        for e in range(half):
            total = sum(p[e].astype(F32) for p in parts)
            out_ref[:, h * half + e, :] = total.T


def shift(x, axis, step, by_core=False):
    owners = lax.axis_size("expert")
    pairs = []
    for n in range(SIDE * SIDE * owners):
        i, j, k = n // owners // SIDE, n // owners % SIDE, n % owners
        by = -step if by_core and k % 2 else step
        i, j = ((i + by) % SIDE, j) if axis == 0 else (i, (j + by) % SIDE)
        pairs.append((n, (i * SIDE + j) * owners + k))
    return lax.ppermute(x, ("dp", "expert"), pairs)


def gather_half(weights, first):
    blocks = [jnp.stack([weights] + [shift(weights, first, -d) for d in range(1, SIDE)])]
    for _ in range(1, SIDE):
        blocks.append(shift(blocks[-1], 1 - first, 1, by_core=True))
    return [pltpu.with_memory_space_constraint(b, pltpu.HBM) for b in blocks]


def add(*parts):
    return sum(p.astype(F32) for p in parts)


def scatter_half(messages, first):
    got = [messages[0]] + [shift(messages[d], first, d) for d in range(1, SIDE)]
    sums = [add(*[g[d] for g in got]).astype(BF16) for d in range(SIDE)]
    return [sums[0]] + [shift(sums[d], 1 - first, d) for d in range(1, SIDE)]


VMEM = pl.BlockSpec(memory_space=pltpu.VMEM)
SMEM = pl.BlockSpec(memory_space=pltpu.SMEM)
ANY = pl.BlockSpec(memory_space=pl.ANY)
HBM = pl.BlockSpec(memory_space=pltpu.HBM)


def params(mib):
    return pltpu.CompilerParams(vmem_limit_bytes=mib * 2**20)


def cost(flops, moved):
    return pl.CostEstimate(flops=int(flops), bytes_accessed=int(moved), transcendentals=0)


def sds(shape, dtype):
    return jax.ShapeDtypeStruct(shape, dtype)


def pack(owners, local, ids, gate, hidden):
    routes, width = hidden.shape
    return pl.pallas_call(
        functools.partial(pack_kernel, owners, local),
        out_shape=[sds((owners, local * CAP + EXTRA, width), BF16), sds(ids.shape, F32)],
        in_specs=[VMEM] * 3,
        out_specs=[VMEM] * 2,
        compiler_params=params(20),
        cost_estimate=cost(2 * owners * local * CAP * routes * width, 2**22),
        name="pack",
    )(ids, gate, hidden)


def expert_call(local, at, wire, grads, pieces):
    owners, tokens, model = grads.shape
    width = wire.shape[2]
    depth = model // (SIDE * SIDE)
    rows = owners * CAP
    return pl.pallas_call(
        functools.partial(expert_kernel, local),
        out_shape=[pltpu.HBM((SIDE, local // 2, width, depth), BF16)] * (2 * SIDE)
        + [pltpu.HBM((owners, local * CAP, width), BF16)],
        in_specs=[SMEM, VMEM] + [HBM] * (1 + len(pieces)),
        out_specs=[HBM] * (2 * SIDE + 1),
        scratch_shapes=[
            pltpu.VMEM((owners, tokens, model), BF16),
            pltpu.VMEM((local, rows, model), BF16),
            pltpu.VMEM((2, SIDE, SIDE, local // 2, width, depth), BF16),
            pltpu.VMEM((2, SIDE, SIDE, local // 2, depth, width), BF16),
            pltpu.VMEM((owners, local * CAP, width), F32),
            pltpu.VMEM((owners, local * CAP, width), BF16),
            pltpu.SemaphoreType.DMA((owners // 2,)),
            pltpu.SemaphoreType.DMA((2, SIDE)),
            pltpu.SemaphoreType.DMA((2, SIDE)),
            pltpu.SemaphoreType.DMA,
        ],
        compiler_params=params(40),
        cost_estimate=cost(6.4e9, 24e6),
        name="experts",
    )(at, wire, pltpu.with_memory_space_constraint(grads, pltpu.HBM), *pieces)


def unpack(ids, pos, gate, hidden, back):
    routes, width = hidden.shape
    return pl.pallas_call(
        unpack_kernel,
        out_shape=[sds((routes, width), BF16), sds(ids.shape, BF16)],
        in_specs=[VMEM] * 5,
        out_specs=[VMEM] * 2,
        compiler_params=params(20),
        cost_estimate=cost(2 * back.shape[0] * routes * width, 2**22),
        name="unpack",
    )(ids, pos, gate, hidden, back)


def finish(parts, after, depth, local, width):
    return pl.pallas_call(
        finish_kernel,
        out_shape=sds((depth, local, width), F32),
        in_specs=[ANY] + [VMEM] * len(parts),
        out_specs=VMEM,
        compiler_params=params(12),
        cost_estimate=cost(2**20, 2.5e6),
        name="finish",
    )(after, *parts)


def per_device(out_grad, saved_hidden, gate_weight, expert_ids, down_weight):
    tokens, top = expert_ids.shape
    width = saved_hidden.shape[2]
    owners = lax.axis_size("expert")
    depth, local, _ = down_weight.shape
    dp = lax.axis_index("dp").astype(I32)
    at = jnp.stack([dp // SIDE, dp % SIDE, lax.axis_index("expert").astype(I32) % 2])
    half = local // 2

    grads = lax.all_gather(out_grad, "expert", axis=0, tiled=False)
    ids, gate = expert_ids.T, gate_weight.T
    hidden = saved_hidden.reshape(tokens * top, width)
    wire, pos = pack(owners, local, ids, gate, hidden)
    wire = lax.all_to_all(wire, "expert", split_axis=0, concat_axis=0, tiled=True)
    weights = down_weight.transpose(1, 0, 2)
    pieces = gather_half(weights[:half], 0) + gather_half(weights[half:], 1)

    *messages, u = expert_call(local, at, wire, grads, pieces)
    back = lax.all_to_all(u, "expert", split_axis=0, concat_axis=0, tiled=True)
    sums = scatter_half(messages[:SIDE], 0) + scatter_half(messages[SIDE:], 1)
    back = back.reshape(owners * local * CAP, width)
    grad_hidden, grad_gate = unpack(ids, pos, gate, hidden, back)
    grad_down = finish(sums, grad_gate, depth, local, width)
    return grad_hidden.reshape(tokens, top, width), grad_gate.T, grad_down


def solution(mesh):
    in_specs = (
        P(("dp", "expert"), None),
        P(("dp", "expert"), None, None),
        P(("dp", "expert"), None),
        P(("dp", "expert"), None),
        P("dp", "expert", None),
    )
    out_specs = (
        P(("dp", "expert"), None, None),
        P(("dp", "expert"), None),
        P("dp", "expert", None),
    )
    return jax.shard_map(
        per_device, mesh=mesh, in_specs=in_specs, out_specs=out_specs, check_vma=False
    )
```

```python
import functools

import jax
import jax.numpy as jnp
from jax import lax
from jax.experimental import pallas as pl
from jax.experimental.pallas import tpu as pltpu
from jax.sharding import PartitionSpec as P

CAP = 24
SIDE = 4
EXTRA = 8
HIDDEN_FLOPS = 2.4e9
SUM_FLOPS = 6e9
BF16, F32, I32 = jnp.bfloat16, jnp.float32, jnp.int32


def iota(shape, dim):
    return lax.broadcasted_iota(I32, shape, dim)


def dot(a, b):
    return jnp.dot(a, b, preferred_element_type=F32)


def add(*parts):
    return sum(p.astype(F32) for p in parts)


def pack_kernel(owners, local, ids_ref, gate_ref, hidden_ref, wire_ref, pos_ref):
    top, tokens = ids_ref.shape
    routes, width = hidden_ref.shape
    experts = owners * local
    ids = ids_ref[...]
    expert_no = iota((experts, tokens), 0)
    named = [expert_no == ids[k : k + 1, :] for k in range(top)]
    member = sum(n.astype(F32) for n in named)
    earlier = (iota((tokens, tokens), 0) < iota((tokens, tokens), 1)).astype(F32).astype(BF16)
    before = dot(member.astype(BF16), earlier)
    pos = jnp.concatenate(
        [jnp.sum(jnp.where(n, before, 0.0), axis=0, keepdims=True) for n in named], axis=0
    )
    pos_ref[...] = pos
    spread = (iota((tokens, routes), 1) // top == iota((tokens, routes), 0)).astype(F32).astype(BF16)
    own = iota((top, routes), 1) % top == iota((top, routes), 0)

    def row(x):
        return jnp.sum(jnp.where(own, dot(x.astype(BF16), spread), 0.0), axis=0, keepdims=True)

    slot_row = row(ids.astype(F32)) * CAP + row(pos)
    gate_row = row(gate_ref[...].astype(F32))
    slots = jnp.where(member > 0.0, before, -1.0).astype(BF16)
    r, c = iota((owners * EXTRA, experts), 0), iota((owners * EXTRA, experts), 1)
    pick = ((r % EXTRA < local) & (c == r // EXTRA * local + r % EXTRA)).astype(F32).astype(BF16)
    slots = dot(pick, slots)
    slots = jnp.concatenate([slots, jnp.zeros((owners * EXTRA, width - tokens), F32)], axis=1)
    rows = local * CAP
    group = 4
    hidden = hidden_ref[...]
    for g in range(owners // group):
        row_no = (iota((group * rows, routes), 0) + g * group * rows).astype(F32)
        onehot = jnp.where(row_no == slot_row, gate_row, 0.0).astype(BF16)
        packed = dot(onehot, hidden)
        for i in range(group):
            o = g * group + i
            wire_ref[o] = jnp.concatenate(
                [packed[i * rows : (i + 1) * rows], slots[o * EXTRA : (o + 1) * EXTRA]], axis=0
            ).astype(BF16)


ROLE = {(0, 2): 0, (1, 1): 1, (1, 2): 2, (0, 3): 3, (0, 1): 4, (1, 3): 5, (0, 0): 6, (1, 0): 7}


def expert_kernel(local, at_ref, wire_ref, grad_hbm, *refs):
    half = local // 2
    refs = refs[2:]
    messages, x_hbm = refs[: 2 * SIDE], refs[2 * SIDE]
    gbuf, xbuf, abuf, gsem, msem, xsem = refs[2 * SIDE + 1 :]
    owners, tokens, model = gbuf.shape
    width = wire_ref.shape[2]
    depth = model // (SIDE * SIDE)
    chips = owners // 2
    loads = [
        pltpu.make_async_copy(grad_hbm.at[pl.ds(2 * p, 2)], gbuf.at[pl.ds(2 * p, 2)], gsem.at[p])
        for p in range(chips)
    ]
    for c in loads:
        c.start()
    places = []
    for d in range(SIDE * SIDE):
        dx = (d // SIDE + SIDE - at_ref[0]) % SIDE
        dy = (d % SIDE + SIDE - at_ref[1]) % SIDE
        places.append(pl.multiple_of((dx * SIDE + dy) * depth, depth))
    block = 2 * CAP
    for p in range(chips):
        slot = [
            wire_ref[2 * p + i, local * CAP : local * CAP + EXTRA, :tokens].astype(F32)
            for i in range(2)
        ]
        slot[1] = jnp.where(slot[1] >= 0.0, slot[1] + CAP, -1.0)
        slot = jnp.concatenate(slot, axis=1)
        onehot = jnp.concatenate(
            [
                (slot[e : e + 1, :] == iota((block, 2 * tokens), 0).astype(F32)).astype(F32)
                for e in range(local)
            ],
            axis=0,
        ).astype(BF16)
        loads[p].wait()
        rows = dot(onehot, gbuf[2 * p : 2 * p + 2].reshape(2 * tokens, model)).astype(BF16)
        for e in range(local):
            for d in range(SIDE * SIDE):
                xbuf[e, p * block : (p + 1) * block, pl.ds(places[d], depth)] = rows[
                    e * block : (e + 1) * block, d * depth : (d + 1) * depth
                ]
    copies = [pltpu.make_async_copy(xbuf, x_hbm, xsem)]
    copies[0].start()
    wire = wire_ref[:, : local * CAP, :].astype(F32)
    step = SIDE * depth
    for e in range(local):
        hidden = wire[:, e * CAP : (e + 1) * CAP, :].reshape(owners * CAP, width)
        hidden = hidden.T.astype(BF16)
        h = e // half
        for dx in range(SIDE):
            grad = dot(hidden, xbuf[e, :, dx * step : (dx + 1) * step]).astype(BF16)
            for dy in range(SIDE):
                a, b = (dx, dy) if h == 0 else (dy, dx)
                abuf[h, ROLE[e % half, a], b] = grad[:, dy * depth : (dy + 1) * depth]
        if e % half == half - 1:
            for m in range(SIDE):
                block_pair = abuf.at[h, pl.ds(2 * m, 2)]
                copies.append(pltpu.make_async_copy(block_pair, messages[h * SIDE + m], msem.at[h, m]))
                copies[-1].start()
    for c in copies:
        c.wait()


def hidden_kernel(local, at_ref, x_hbm, *refs):
    half = local // 2
    pieces, refs = refs[: 2 * SIDE], refs[2 * SIDE :]
    u_hbm, xbuf, wbuf, ubuf, obuf, xsem, wsem, usem = refs
    owners, _, width = ubuf.shape
    step = xbuf.shape[2] // SIDE
    rows = [pltpu.make_async_copy(x_hbm.at[e], xbuf.at[e], xsem.at[e]) for e in range(local)]
    weights = [
        [
            pltpu.make_async_copy(
                pieces[h * SIDE + k],
                wbuf.at[h, at_ref[2] * k + (1 - at_ref[2]) * ((SIDE - k) % SIDE)],
                wsem.at[h, k],
            )
            for k in range(SIDE)
        ]
        for h in range(2)
    ]
    for h in range(2):
        for c in weights[h] + rows[h * half : (h + 1) * half]:
            c.start()
    for e in range(local):
        h = e // half
        rows[e].wait()
        if e % half == 0:
            for c in weights[h]:
                c.wait()
        u = jnp.zeros((owners * CAP, width), F32)
        for dx in range(SIDE):
            w = wbuf[0, :, dx, e % half] if h == 0 else wbuf[1, dx, :, e % half]
            u += dot(xbuf[e, :, dx * step : (dx + 1) * step], w.reshape(step, width))
        ubuf[:, e * CAP : (e + 1) * CAP, :] = u.reshape(owners, CAP, width)
    obuf[...] = ubuf[...].astype(BF16)
    out = pltpu.make_async_copy(obuf, u_hbm, usem)
    out.start()
    out.wait()


def unpack_kernel(ids_ref, pos_ref, gate_ref, hidden_ref, back_ref, out_ref, gate_out_ref):
    top, tokens = ids_ref.shape
    routes, width = hidden_ref.shape
    slots = back_ref.shape[0]
    spread = (iota((routes, tokens), 0) // top == iota((routes, tokens), 1)).astype(F32).astype(BF16)
    own = iota((routes, top), 0) % top == iota((routes, top), 1)

    def column(x):
        y = lax.dot_general(spread, x.astype(BF16), (((1,), (1,)), ((), ())), preferred_element_type=F32)
        return jnp.sum(jnp.where(own, y, 0.0), axis=1, keepdims=True)

    slot = column(ids_ref[...].astype(F32)) * CAP + column(pos_ref[...])
    gate = column(gate_ref[...].astype(F32))
    back = back_ref[...]
    part = routes // 4
    grads = []
    for p in range(4):
        here = slice(p * part, (p + 1) * part)
        onehot = (iota((part, slots), 1).astype(F32) == slot[here]).astype(F32).astype(BF16)
        rows = dot(onehot, back)
        out_ref[here, :] = (rows * gate[here]).astype(BF16)
        grads.append(jnp.sum(rows * hidden_ref[here, :].astype(F32), axis=1, keepdims=True))
    grad = jnp.where(own, jnp.concatenate(grads, axis=0), 0.0).astype(BF16)
    gate_out_ref[...] = lax.dot_general(
        grad, spread, (((0,), (0,)), ((), ())), preferred_element_type=F32
    ).astype(BF16)


def sum_kernel(*refs):
    for h in range(2):
        own, on, back, on_later, back_later = refs[5 * h : 5 * h + 5]
        outs = refs[10 + SIDE * h : 10 + SIDE * (h + 1)]
        for d in range(SIDE):
            outs[d][0] = add(own[0, d], back[1, d], on_later[d]).astype(BF16)
            outs[d][1] = add(own[1, d], on[1, d], back_later[d]).astype(BF16)


def finish_kernel(after_ref, *refs):
    out_ref = refs[-1]
    half = out_ref.shape[1] // 2
    for h in range(2):
        parts = refs[h * SIDE : (h + 1) * SIDE]
        for e in range(half):
            total = sum(p[e].astype(F32) for p in parts)
            out_ref[:, h * half + e, :] = total.T


def shift(x, axis, step, by_core=False):
    owners = lax.axis_size("expert")
    pairs = []
    for n in range(SIDE * SIDE * owners):
        i, j, k = n // owners // SIDE, n // owners % SIDE, n % owners
        by = -step if by_core and k % 2 else step
        i, j = ((i + by) % SIDE, j) if axis == 0 else (i, (j + by) % SIDE)
        pairs.append((n, (i * SIDE + j) * owners + k))
    return lax.ppermute(x, ("dp", "expert"), pairs)


def gather_half(weights, first):
    blocks = [jnp.stack([weights] + [shift(weights, first, -d) for d in range(1, SIDE)])]
    for _ in range(1, SIDE):
        blocks.append(shift(blocks[-1], 1 - first, 1, by_core=True))
    return [pltpu.with_memory_space_constraint(b, pltpu.HBM) for b in blocks]


def scatter(messages):
    got = []
    for h in range(2):
        on, back, later, own = messages[h]
        on, back = shift(on, h, 1), shift(back, h, -1)
        on_later = shift(add(later[0], on[0]).astype(BF16), h, 1)
        back_later = shift(add(later[1], back[0]).astype(BF16), h, -1)
        got += [own, on, back, on_later, back_later]
    sums = sum_call(got)
    out = []
    for h in range(2):
        mine = sums[h * SIDE : (h + 1) * SIDE]
        out += [mine[0]] + [shift(mine[d], 1 - h, d) for d in range(1, SIDE)]
    return out


VMEM = pl.BlockSpec(memory_space=pltpu.VMEM)
SMEM = pl.BlockSpec(memory_space=pltpu.SMEM)
ANY = pl.BlockSpec(memory_space=pl.ANY)
HBM = pl.BlockSpec(memory_space=pltpu.HBM)


def params(mib):
    return pltpu.CompilerParams(vmem_limit_bytes=mib * 2**20)


def cost(flops, moved):
    return pl.CostEstimate(flops=int(flops), bytes_accessed=int(moved), transcendentals=0)


def sds(shape, dtype):
    return jax.ShapeDtypeStruct(shape, dtype)


def pack(owners, local, ids, gate, hidden):
    routes, width = hidden.shape
    return pl.pallas_call(
        functools.partial(pack_kernel, owners, local),
        out_shape=[sds((owners, local * CAP + EXTRA, width), BF16), sds(ids.shape, F32)],
        in_specs=[VMEM] * 3,
        out_specs=[VMEM] * 2,
        compiler_params=params(20),
        cost_estimate=cost(2 * owners * local * CAP * routes * width, 2**22),
        name="pack",
    )(ids, gate, hidden)


def expert_call(local, at, wire, grads, after):
    owners, tokens, model = grads.shape
    width = wire.shape[2]
    depth = model // (SIDE * SIDE)
    rows = owners * CAP
    return pl.pallas_call(
        functools.partial(expert_kernel, local),
        out_shape=[pltpu.HBM((2, SIDE, width, depth), BF16)] * (2 * SIDE)
        + [pltpu.HBM((local, rows, model), BF16)],
        in_specs=[SMEM, VMEM, HBM] + [HBM] * len(after),
        out_specs=[HBM] * (2 * SIDE + 1),
        scratch_shapes=[
            pltpu.VMEM((owners, tokens, model), BF16),
            pltpu.VMEM((local, rows, model), BF16),
            pltpu.VMEM((2, 2 * SIDE, SIDE, width, depth), BF16),
            pltpu.SemaphoreType.DMA((owners // 2,)),
            pltpu.SemaphoreType.DMA((2, SIDE)),
            pltpu.SemaphoreType.DMA,
        ],
        compiler_params=params(36),
        cost_estimate=cost(4e9, 22e6),
        name="experts",
    )(at, wire, pltpu.with_memory_space_constraint(grads, pltpu.HBM), *after)


def hidden_call(local, at, x, pieces):
    _, rows, model = x.shape
    depth, width = pieces[0].shape[2:]
    owners = rows // CAP
    return pl.pallas_call(
        functools.partial(hidden_kernel, local),
        out_shape=pltpu.HBM((owners, local * CAP, width), BF16),
        in_specs=[SMEM] + [HBM] * (1 + len(pieces)),
        out_specs=HBM,
        scratch_shapes=[
            pltpu.VMEM((local, rows, model), BF16),
            pltpu.VMEM((2, SIDE, SIDE, local // 2, depth, width), BF16),
            pltpu.VMEM((owners, local * CAP, width), F32),
            pltpu.VMEM((owners, local * CAP, width), BF16),
            pltpu.SemaphoreType.DMA((local,)),
            pltpu.SemaphoreType.DMA((2, SIDE)),
            pltpu.SemaphoreType.DMA,
        ],
        compiler_params=params(28),
        cost_estimate=cost(HIDDEN_FLOPS, 14e6),
        name="hidden_grad",
    )(at, x, *pieces)


def sum_call(parts):
    _, _, width, depth = parts[0].shape
    return pl.pallas_call(
        sum_kernel,
        out_shape=[sds((2, width, depth), BF16)] * (2 * SIDE),
        in_specs=[VMEM] * len(parts),
        out_specs=[VMEM] * (2 * SIDE),
        compiler_params=params(24),
        cost_estimate=cost(SUM_FLOPS, 4e6),
        name="sum_parts",
    )(*parts)


def unpack(ids, pos, gate, hidden, back):
    routes, width = hidden.shape
    return pl.pallas_call(
        unpack_kernel,
        out_shape=[sds((routes, width), BF16), sds(ids.shape, BF16)],
        in_specs=[VMEM] * 5,
        out_specs=[VMEM] * 2,
        compiler_params=params(20),
        cost_estimate=cost(2 * back.shape[0] * routes * width, 2**22),
        name="unpack",
    )(ids, pos, gate, hidden, back)


def finish(parts, after, depth, local, width):
    return pl.pallas_call(
        finish_kernel,
        out_shape=sds((depth, local, width), F32),
        in_specs=[ANY] + [VMEM] * len(parts),
        out_specs=VMEM,
        compiler_params=params(12),
        cost_estimate=cost(2**20, 2.5e6),
        name="finish",
    )(after, *parts)


def per_device(out_grad, saved_hidden, gate_weight, expert_ids, down_weight):
    tokens, top = expert_ids.shape
    width = saved_hidden.shape[2]
    owners = lax.axis_size("expert")
    depth, local, _ = down_weight.shape
    dp = lax.axis_index("dp").astype(I32)
    at = jnp.stack([dp // SIDE, dp % SIDE, lax.axis_index("expert").astype(I32) % 2])
    half = local // 2

    grads = lax.all_gather(out_grad, "expert", axis=0, tiled=False)
    ids, gate = expert_ids.T, gate_weight.T
    hidden = saved_hidden.reshape(tokens * top, width)
    wire, pos = pack(owners, local, ids, gate, hidden)
    wire = lax.all_to_all(wire, "expert", split_axis=0, concat_axis=0, tiled=True)
    weights = down_weight.transpose(1, 0, 2)
    pieces = gather_half(weights[:half], 0) + gather_half(weights[half:], 1)

    *messages, x = expert_call(local, at, wire, grads, (pieces[SIDE - 1], pieces[-1]))
    u = hidden_call(local, at, x, pieces)
    back = lax.all_to_all(u, "expert", split_axis=0, concat_axis=0, tiled=True)
    sums = scatter((messages[:SIDE], messages[SIDE:]))
    back = back.reshape(owners * local * CAP, width)
    grad_hidden, grad_gate = unpack(ids, pos, gate, hidden, back)
    grad_down = finish(sums, grad_gate, depth, local, width)
    return grad_hidden.reshape(tokens, top, width), grad_gate.T, grad_down


def solution(mesh):
    in_specs = (
        P(("dp", "expert"), None),
        P(("dp", "expert"), None, None),
        P(("dp", "expert"), None),
        P(("dp", "expert"), None),
        P("dp", "expert", None),
    )
    out_specs = (
        P(("dp", "expert"), None, None),
        P(("dp", "expert"), None),
        P("dp", "expert", None),
    )
    return jax.shard_map(
        per_device, mesh=mesh, in_specs=in_specs, out_specs=out_specs, check_vma=False
    )
```

```python
import functools

import jax
import jax.numpy as jnp
from jax import lax
from jax.experimental import pallas as pl
from jax.experimental.pallas import tpu as pltpu
from jax.sharding import PartitionSpec as P

CAP = 24
SIDE = 4
EXTRA = 8
HIDDEN_FLOPS = 2.4e9
SUM_FLOPS = 6e9
BF16, F32, I32 = jnp.bfloat16, jnp.float32, jnp.int32


def iota(shape, dim):
    return lax.broadcasted_iota(I32, shape, dim)


def dot(a, b):
    return jnp.dot(a, b, preferred_element_type=F32)


def add(*parts):
    return sum(p.astype(F32) for p in parts)


def pack_kernel(owners, local, ids_ref, gate_ref, hidden_ref, wire_ref, pos_ref):
    top, tokens = ids_ref.shape
    routes, width = hidden_ref.shape
    experts = owners * local
    ids = ids_ref[...]
    expert_no = iota((experts, tokens), 0)
    named = [expert_no == ids[k : k + 1, :] for k in range(top)]
    member = sum(n.astype(F32) for n in named)
    earlier = (iota((tokens, tokens), 0) < iota((tokens, tokens), 1)).astype(F32).astype(BF16)
    before = dot(member.astype(BF16), earlier)
    pos = jnp.concatenate(
        [jnp.sum(jnp.where(n, before, 0.0), axis=0, keepdims=True) for n in named], axis=0
    )
    pos_ref[...] = pos
    spread = (iota((tokens, routes), 1) // top == iota((tokens, routes), 0)).astype(F32).astype(BF16)
    own = iota((top, routes), 1) % top == iota((top, routes), 0)

    def row(x):
        return jnp.sum(jnp.where(own, dot(x.astype(BF16), spread), 0.0), axis=0, keepdims=True)

    slot_row = row(ids.astype(F32)) * CAP + row(pos)
    gate_row = row(gate_ref[...].astype(F32))
    slots = jnp.where(member > 0.0, before, -1.0).astype(BF16)
    r, c = iota((owners * EXTRA, experts), 0), iota((owners * EXTRA, experts), 1)
    pick = ((r % EXTRA < local) & (c == r // EXTRA * local + r % EXTRA)).astype(F32).astype(BF16)
    slots = dot(pick, slots)
    slots = jnp.concatenate([slots, jnp.zeros((owners * EXTRA, width - tokens), F32)], axis=1)
    rows = local * CAP
    group = 4
    hidden = hidden_ref[...]
    for g in range(owners // group):
        row_no = (iota((group * rows, routes), 0) + g * group * rows).astype(F32)
        onehot = jnp.where(row_no == slot_row, gate_row, 0.0).astype(BF16)
        packed = dot(onehot, hidden)
        for i in range(group):
            o = g * group + i
            wire_ref[o] = jnp.concatenate(
                [packed[i * rows : (i + 1) * rows], slots[o * EXTRA : (o + 1) * EXTRA]], axis=0
            ).astype(BF16)


ROLE = {(0, 2): 0, (1, 1): 1, (1, 2): 2, (0, 3): 3, (0, 1): 4, (1, 3): 5, (0, 0): 6, (1, 0): 7}


def expert_kernel(local, at_ref, wire_ref, grad_hbm, *refs):
    half = local // 2
    refs = refs[2:]
    messages, x_hbm = refs[: 2 * SIDE], refs[2 * SIDE]
    gbuf, xbuf, abuf, gsem, msem, xsem = refs[2 * SIDE + 1 :]
    owners, tokens, model = gbuf.shape
    width = wire_ref.shape[2]
    depth = model // (SIDE * SIDE)
    chips = owners // 2
    loads = [
        pltpu.make_async_copy(grad_hbm.at[pl.ds(2 * p, 2)], gbuf.at[pl.ds(2 * p, 2)], gsem.at[p])
        for p in range(chips)
    ]
    for c in loads:
        c.start()
    places = []
    for d in range(SIDE * SIDE):
        dx = (d // SIDE + SIDE - at_ref[0]) % SIDE
        dy = (d % SIDE + SIDE - at_ref[1]) % SIDE
        places.append(pl.multiple_of((dx * SIDE + dy) * depth, depth))
    block = 2 * CAP
    for p in range(chips):
        slot = [
            wire_ref[2 * p + i, local * CAP : local * CAP + EXTRA, :tokens].astype(F32)
            for i in range(2)
        ]
        slot[1] = jnp.where(slot[1] >= 0.0, slot[1] + CAP, -1.0)
        slot = jnp.concatenate(slot, axis=1)
        onehot = jnp.concatenate(
            [
                (slot[e : e + 1, :] == iota((block, 2 * tokens), 0).astype(F32)).astype(F32)
                for e in range(local)
            ],
            axis=0,
        ).astype(BF16)
        loads[p].wait()
        rows = dot(onehot, gbuf[2 * p : 2 * p + 2].reshape(2 * tokens, model)).astype(BF16)
        for e in range(local):
            for d in range(SIDE * SIDE):
                xbuf[e, p * block : (p + 1) * block, pl.ds(places[d], depth)] = rows[
                    e * block : (e + 1) * block, d * depth : (d + 1) * depth
                ]
    copies = [pltpu.make_async_copy(xbuf, x_hbm, xsem)]
    copies[0].start()
    wire = wire_ref[:, : local * CAP, :].astype(F32)
    step = SIDE * depth
    for e in range(local):
        hidden = wire[:, e * CAP : (e + 1) * CAP, :].reshape(owners * CAP, width)
        hidden = hidden.T.astype(BF16)
        h = e // half
        for dx in range(SIDE):
            grad = dot(hidden, xbuf[e, :, dx * step : (dx + 1) * step]).astype(BF16)
            for dy in range(SIDE):
                a, b = (dx, dy) if h == 0 else (dy, dx)
                abuf[h, ROLE[e % half, a], b] = grad[:, dy * depth : (dy + 1) * depth]
        if e % half == half - 1:
            for m in range(SIDE):
                block_pair = abuf.at[h, pl.ds(2 * m, 2)]
                copies.append(pltpu.make_async_copy(block_pair, messages[h * SIDE + m], msem.at[h, m]))
                copies[-1].start()
    for c in copies:
        c.wait()


def hidden_kernel(local, at_ref, x_hbm, *refs):
    half = local // 2
    pieces, refs = refs[: 2 * SIDE], refs[2 * SIDE :]
    u_hbm, xbuf, wbuf, ubuf, obuf, xsem, wsem, usem = refs
    owners, _, width = ubuf.shape
    step = xbuf.shape[2] // SIDE
    rows = [pltpu.make_async_copy(x_hbm.at[e], xbuf.at[e], xsem.at[e]) for e in range(local)]
    weights = [
        [
            pltpu.make_async_copy(
                pieces[h * SIDE + k],
                wbuf.at[h, at_ref[2] * k + (1 - at_ref[2]) * ((SIDE - k) % SIDE)],
                wsem.at[h, k],
            )
            for k in range(SIDE)
        ]
        for h in range(2)
    ]
    for h in range(2):
        for c in weights[h] + rows[h * half : (h + 1) * half]:
            c.start()
    for e in range(local):
        h = e // half
        rows[e].wait()
        if e % half == 0:
            for c in weights[h]:
                c.wait()
        u = jnp.zeros((owners * CAP, width), F32)
        for dx in range(SIDE):
            w = wbuf[0, :, dx, e % half] if h == 0 else wbuf[1, dx, :, e % half]
            u += dot(xbuf[e, :, dx * step : (dx + 1) * step], w.reshape(step, width))
        ubuf[:, e * CAP : (e + 1) * CAP, :] = u.reshape(owners, CAP, width)
    obuf[...] = ubuf[...].astype(BF16)
    out = pltpu.make_async_copy(obuf, u_hbm, usem)
    out.start()
    out.wait()


def unpack_kernel(ids_ref, pos_ref, gate_ref, hidden_ref, back_ref, out_ref, gate_out_ref):
    top, tokens = ids_ref.shape
    routes, width = hidden_ref.shape
    slots = back_ref.shape[0]
    spread = (iota((routes, tokens), 0) // top == iota((routes, tokens), 1)).astype(F32).astype(BF16)
    own = iota((routes, top), 0) % top == iota((routes, top), 1)

    def column(x):
        y = lax.dot_general(spread, x.astype(BF16), (((1,), (1,)), ((), ())), preferred_element_type=F32)
        return jnp.sum(jnp.where(own, y, 0.0), axis=1, keepdims=True)

    slot = column(ids_ref[...].astype(F32)) * CAP + column(pos_ref[...])
    gate = column(gate_ref[...].astype(F32))
    back = back_ref[...]
    part = routes // 4
    grads = []
    for p in range(4):
        here = slice(p * part, (p + 1) * part)
        onehot = (iota((part, slots), 1).astype(F32) == slot[here]).astype(F32).astype(BF16)
        rows = dot(onehot, back)
        out_ref[here, :] = (rows * gate[here]).astype(BF16)
        grads.append(jnp.sum(rows * hidden_ref[here, :].astype(F32), axis=1, keepdims=True))
    grad = jnp.where(own, jnp.concatenate(grads, axis=0), 0.0).astype(BF16)
    gate_out_ref[...] = lax.dot_general(
        grad, spread, (((0,), (0,)), ((), ())), preferred_element_type=F32
    ).astype(BF16)


def sum_kernel(*refs):
    kept, sem = refs[10 + 2 * SIDE :]
    copies = []
    for h in range(2):
        own, on, back, on_later, back_later = refs[5 * h : 5 * h + 5]
        outs = refs[10 + SIDE * h : 10 + SIDE * (h + 1)]
        for d in range(SIDE):
            first = add(own[0, d], back[1, d], on_later[d]).astype(BF16)
            second = add(own[1, d], on[1, d], back_later[d]).astype(BF16)
            if d == 0:
                kept[h, 0] = first
                kept[h, 1] = second
                copies.append(pltpu.make_async_copy(kept.at[h], outs[0], sem.at[h]))
                copies[-1].start()
            else:
                outs[d][0] = first
                outs[d][1] = second
    for c in copies:
        c.wait()


def finish_kernel(after_ref, *refs):
    out_ref = refs[-1]
    half = out_ref.shape[1] // 2
    for h in range(2):
        parts = refs[h * SIDE : (h + 1) * SIDE]
        for e in range(half):
            total = sum(p[e].astype(F32) for p in parts)
            out_ref[:, h * half + e, :] = total.T


def shift(x, axis, step, by_core=False):
    owners = lax.axis_size("expert")
    pairs = []
    for n in range(SIDE * SIDE * owners):
        i, j, k = n // owners // SIDE, n // owners % SIDE, n % owners
        by = -step if by_core and k % 2 else step
        i, j = ((i + by) % SIDE, j) if axis == 0 else (i, (j + by) % SIDE)
        pairs.append((n, (i * SIDE + j) * owners + k))
    return lax.ppermute(x, ("dp", "expert"), pairs)


def gather_half(weights, first):
    blocks = [jnp.stack([weights] + [shift(weights, first, -d) for d in range(1, SIDE)])]
    for _ in range(1, SIDE):
        blocks.append(shift(blocks[-1], 1 - first, 1, by_core=True))
    return [pltpu.with_memory_space_constraint(b, pltpu.HBM) for b in blocks]


def scatter(messages):
    got = []
    for h in range(2):
        on, back, later, own = messages[h]
        on, back = shift(on, h, 1), shift(back, h, -1)
        on_later = shift(add(later[0], on[0]).astype(BF16), h, 1)
        back_later = shift(add(later[1], back[0]).astype(BF16), h, -1)
        got += [own, on, back, on_later, back_later]
    sums = sum_call(got)
    out = []
    for h in range(2):
        mine = sums[h * SIDE : (h + 1) * SIDE]
        out += [mine[0]] + [shift(mine[d], 1 - h, d) for d in range(1, SIDE)]
    return out


VMEM = pl.BlockSpec(memory_space=pltpu.VMEM)
SMEM = pl.BlockSpec(memory_space=pltpu.SMEM)
ANY = pl.BlockSpec(memory_space=pl.ANY)
HBM = pl.BlockSpec(memory_space=pltpu.HBM)


def params(mib):
    return pltpu.CompilerParams(vmem_limit_bytes=mib * 2**20)


def cost(flops, moved):
    return pl.CostEstimate(flops=int(flops), bytes_accessed=int(moved), transcendentals=0)


def sds(shape, dtype):
    return jax.ShapeDtypeStruct(shape, dtype)


def pack(owners, local, ids, gate, hidden):
    routes, width = hidden.shape
    return pl.pallas_call(
        functools.partial(pack_kernel, owners, local),
        out_shape=[sds((owners, local * CAP + EXTRA, width), BF16), sds(ids.shape, F32)],
        in_specs=[VMEM] * 3,
        out_specs=[VMEM] * 2,
        compiler_params=params(20),
        cost_estimate=cost(2 * owners * local * CAP * routes * width, 2**22),
        name="pack",
    )(ids, gate, hidden)


def expert_call(local, at, wire, grads, after):
    owners, tokens, model = grads.shape
    width = wire.shape[2]
    depth = model // (SIDE * SIDE)
    rows = owners * CAP
    return pl.pallas_call(
        functools.partial(expert_kernel, local),
        out_shape=[pltpu.HBM((2, SIDE, width, depth), BF16)] * (2 * SIDE)
        + [pltpu.HBM((local, rows, model), BF16)],
        in_specs=[SMEM, VMEM, HBM] + [HBM] * len(after),
        out_specs=[HBM] * (2 * SIDE + 1),
        scratch_shapes=[
            pltpu.VMEM((owners, tokens, model), BF16),
            pltpu.VMEM((local, rows, model), BF16),
            pltpu.VMEM((2, 2 * SIDE, SIDE, width, depth), BF16),
            pltpu.SemaphoreType.DMA((owners // 2,)),
            pltpu.SemaphoreType.DMA((2, SIDE)),
            pltpu.SemaphoreType.DMA,
        ],
        compiler_params=params(36),
        cost_estimate=cost(4e9, 22e6),
        name="experts",
    )(at, wire, pltpu.with_memory_space_constraint(grads, pltpu.HBM), *after)


def hidden_call(local, at, x, pieces):
    _, rows, model = x.shape
    depth, width = pieces[0].shape[2:]
    owners = rows // CAP
    return pl.pallas_call(
        functools.partial(hidden_kernel, local),
        out_shape=pltpu.HBM((owners, local * CAP, width), BF16),
        in_specs=[SMEM] + [HBM] * (1 + len(pieces)),
        out_specs=HBM,
        scratch_shapes=[
            pltpu.VMEM((local, rows, model), BF16),
            pltpu.VMEM((2, SIDE, SIDE, local // 2, depth, width), BF16),
            pltpu.VMEM((owners, local * CAP, width), F32),
            pltpu.VMEM((owners, local * CAP, width), BF16),
            pltpu.SemaphoreType.DMA((local,)),
            pltpu.SemaphoreType.DMA((2, SIDE)),
            pltpu.SemaphoreType.DMA,
        ],
        compiler_params=params(28),
        cost_estimate=cost(HIDDEN_FLOPS, 14e6),
        name="hidden_grad",
    )(at, pltpu.with_memory_space_constraint(x, pltpu.HBM), *pieces)


def sum_call(parts):
    _, _, width, depth = parts[0].shape
    return pl.pallas_call(
        sum_kernel,
        out_shape=([pltpu.HBM((2, width, depth), BF16)] + [sds((2, width, depth), BF16)] * (SIDE - 1)) * 2,
        in_specs=[VMEM] * len(parts),
        out_specs=([HBM] + [VMEM] * (SIDE - 1)) * 2,
        scratch_shapes=[pltpu.VMEM((2, 2, width, depth), BF16), pltpu.SemaphoreType.DMA((2,))],
        compiler_params=params(24),
        cost_estimate=cost(SUM_FLOPS, 4e6),
        name="sum_parts",
    )(*parts)


def unpack(ids, pos, gate, hidden, back):
    routes, width = hidden.shape
    return pl.pallas_call(
        unpack_kernel,
        out_shape=[sds((routes, width), BF16), sds(ids.shape, BF16)],
        in_specs=[VMEM] * 5,
        out_specs=[VMEM] * 2,
        compiler_params=params(20),
        cost_estimate=cost(2 * back.shape[0] * routes * width, 2**22),
        name="unpack",
    )(ids, pos, gate, hidden, back)


def finish(parts, after, depth, local, width):
    return pl.pallas_call(
        finish_kernel,
        out_shape=sds((depth, local, width), F32),
        in_specs=[HBM] + [VMEM] * len(parts),
        out_specs=VMEM,
        compiler_params=params(12),
        cost_estimate=cost(2**20, 2.5e6),
        name="finish",
    )(pltpu.with_memory_space_constraint(after, pltpu.HBM), *parts)


def per_device(out_grad, saved_hidden, gate_weight, expert_ids, down_weight):
    tokens, top = expert_ids.shape
    width = saved_hidden.shape[2]
    owners = lax.axis_size("expert")
    depth, local, _ = down_weight.shape
    dp = lax.axis_index("dp").astype(I32)
    at = jnp.stack([dp // SIDE, dp % SIDE, lax.axis_index("expert").astype(I32) % 2])
    half = local // 2

    grads = lax.all_gather(out_grad, "expert", axis=0, tiled=False)
    ids, gate = expert_ids.T, gate_weight.T
    hidden = saved_hidden.reshape(tokens * top, width)
    wire, pos = pack(owners, local, ids, gate, hidden)
    wire = lax.all_to_all(wire, "expert", split_axis=0, concat_axis=0, tiled=True)
    weights = down_weight.transpose(1, 0, 2)
    pieces = gather_half(weights[:half], 0) + gather_half(weights[half:], 1)

    *messages, x = expert_call(local, at, wire, grads, (pieces[SIDE - 1], pieces[-1]))
    u = hidden_call(local, at, x, pieces)
    back = lax.all_to_all(u, "expert", split_axis=0, concat_axis=0, tiled=True)
    sums = scatter((messages[:SIDE], messages[SIDE:]))
    back = back.reshape(owners * local * CAP, width)
    grad_hidden, grad_gate = unpack(ids, pos, gate, hidden, back)
    grad_down = finish(sums, grad_gate, depth, local, width)
    return grad_hidden.reshape(tokens, top, width), grad_gate.T, grad_down


def solution(mesh):
    in_specs = (
        P(("dp", "expert"), None),
        P(("dp", "expert"), None, None),
        P(("dp", "expert"), None),
        P(("dp", "expert"), None),
        P("dp", "expert", None),
    )
    out_specs = (
        P(("dp", "expert"), None, None),
        P(("dp", "expert"), None),
        P("dp", "expert", None),
    )
    return jax.shard_map(
        per_device, mesh=mesh, in_specs=in_specs, out_specs=out_specs, check_vma=False
    )
```
